32 devices in a mesh: dom: 32 (over z, y, x, core).
Axes of the slice: x: 2, y: 2, z: 4, core: 2. Of those that a mesh axis runs over, the one named last changes fastest.
Arguments:
- particles: float32 [32, 2, 256, 128], P('dom'), may hold values from -60 to 60
- offspring: int32 [32], P('dom'), may hold values from 0 to 7, as said below
- noise: float32 [2, 32, 2, 256, 128], P(None, 'dom'), may hold values from -6 to 6
- accept: int32 [2, 32], P(None, 'dom'), may hold values 0 or 1
- observed: float32 [256, 256], replicated, may hold values from -6 to 6
Outputs:
- moved: float32 [32, 2, 256, 128], P('dom')
- misfit: float32 [2, 32], P(None, 'dom')
The draws below stay inside these ranges and needn't reach their ends.
Inputs may be any that keep to these rules, and one draw needn't show every extreme that they name: `offspring`: the counts sum to 32. Slot s, numbered by the counts' running sum, is filled by a particle at most 3 places from s, and in every draw some slot is filled from exactly 3 places away.
All inputs are finite; a program needn't handle non-finite values. No bound on the sum of `accept` on one device may be relied on, other than what follows from the above.
Results may differ from the reference program's by a relative error of at most 0.0001.
Values sent between devices are 32-bit elements; how exact they have to be, the bound alone decides.
A program may use at most 64 MiB of HBM per device.

```python
import jax
import jax.numpy as jnp
from jax import lax

G = 256
HALF = 128
MOVES = 2
STEPS = 1
LOW = 16
PARTICLES = 32
REACH = 3


def draw_particles(key, part):
    index_y = jnp.arange(G)
    wave_y = jnp.where(index_y < G // 2, index_y, index_y - G).astype(jnp.float32)
    wave_x = jnp.arange(G // 2).astype(jnp.float32)
    radius = jnp.sqrt(wave_y[:, None] ** 2 + wave_x[None, :] ** 2)
    spectrum = 1.5 / (1.0 + radius / 8.0)
    order = jnp.arange(PARTICLES).astype(jnp.float32) / max(PARTICLES - 1, 1)
    values = jax.random.normal(key, (PARTICLES, 2, G, G // 2), jnp.float32)
    rising = 1.0 + 2.0 * order
    return values * spectrum[None, None] * rising[:, None, None, None]


def draw_offspring(key, part):
    jumps = 4 * (jax.random.randint(jax.random.fold_in(key, 7), (PARTICLES,), 0, 4) == 0).astype(jnp.int32)
    walker = jnp.cumsum(jumps).astype(jnp.int32) - 2
    slot_ids = jnp.arange(PARTICLES, dtype=jnp.int32)
    base = jnp.clip(jnp.clip(walker, slot_ids - REACH, slot_ids + REACH), 0, PARTICLES - 1)
    center = jax.random.randint(jax.random.fold_in(key, 11), (), REACH, PARTICLES - REACH).astype(jnp.int32)
    source = jnp.where(jnp.abs(slot_ids - center) <= REACH, center, base).astype(jnp.int32)
    return jnp.zeros((PARTICLES,), jnp.int32).at[source].add(1)


def touch_ends(entries, own_key, low, high):
    shape = entries.shape
    spot = [jax.random.randint(jax.random.fold_in(own_key, axis), (), 0, shape[axis]) for axis in range(len(shape))]
    entries = entries.at[tuple(spot)].set(low)
    longest = shape.index(max(shape))
    spot[longest] = (spot[longest] + 1) % shape[longest]
    return entries.at[tuple(spot)].set(high)


def level_of(own_key, shape, cuts, smallest, largest):
    gain = 1.0
    for axis_at, shards_of in cuts:
        steps = jax.random.uniform(jax.random.fold_in(jax.random.fold_in(own_key, 6), axis_at), (shards_of,), jnp.float32, smallest / len(cuts), largest / len(cuts))
        gain = gain * jnp.repeat(jnp.exp(steps), shape[axis_at] // shards_of).reshape((-1,) + (1,) * (len(shape) - 1 - axis_at))
    return gain


def scatter_about(key, dims, scale, bound, pieces=(), held_as=jnp.bfloat16):
    result = scale * jax.random.normal(key, dims, jnp.float32)
    if pieces:
        result = result * level_of(key, dims, pieces, -0.22, 0.18)
    return jnp.clip(result, -bound, bound).astype(held_as)


def setup_inputs(seed: int = 0) -> dict:
    seeds = jax.random.split(jax.random.key(seed), 6)
    particles = draw_particles(jax.random.fold_in(seeds[5], 71), 0)
    offspring = draw_offspring(jax.random.fold_in(seeds[5], 71), 0)
    noise = scatter_about(seeds[2], (MOVES, PARTICLES, 2, G, HALF), 1.0, 6.0, ((1, 32),), jnp.float32)
    accept = touch_ends((jax.random.randint(seeds[3], (MOVES, PARTICLES), 0, 2) < 1).astype(jnp.int32), jax.random.fold_in(seeds[3], 1), 0, 1)
    observed = scatter_about(seeds[4], (G, G), 1.0, 6.0, (), jnp.float32)
    return dict(particles=particles, offspring=offspring, noise=noise, accept=accept, observed=observed)


time_step = 0.05
viscosity = 0.001
noise_level = 0.5
spectral_scale = 64.0
prior_amplitude = 1.5
step_size = 0.4

def wavenumbers():
    index_y = jnp.arange(G)
    wave_y = jnp.where(index_y < G // 2, index_y, index_y - G).astype(jnp.float32)
    wave_x = jnp.arange(G // 2).astype(jnp.float32)
    return (wave_y[:, None], wave_x[None, :])

def synthesize(coeffs):
    padded = jnp.pad(coeffs, ((0, 0), (0, 1)))
    return jnp.fft.irfft2(padded, s=(G, G)) * (G * G / spectral_scale)

def analyse(field):
    return jnp.fft.rfft2(field)[:, :G // 2] * (spectral_scale / (G * G))

def predicted_state(present_state, observed):
    wave_y, wave_x = wavenumbers()
    wave_sq = wave_y * wave_y + wave_x * wave_x
    inverse_sq = jnp.where(wave_sq > 0, 1.0 / jnp.maximum(wave_sq, 1.0), 0.0)
    keeper = ((jnp.abs(wave_y) <= G // 3) & (wave_x <= G // 3)).astype(jnp.float32)
    coeffs = lax.complex(present_state[0], present_state[1])
    for substep in range(STEPS):
        vort = synthesize(coeffs)
        stream = coeffs * inverse_sq
        vel_u = synthesize(1j * wave_y * stream)
        vel_v = synthesize(-1j * wave_x * stream)
        flux_u = analyse(vel_u * vort)
        flux_v = analyse(vel_v * vort)
        nonlin = (1j * wave_x * flux_u + 1j * wave_y * flux_v) * keeper
        coeffs = (coeffs - time_step * nonlin) / (1.0 + time_step * viscosity * wave_sq)
    final = synthesize(coeffs)
    return jnp.sum((final - observed) ** 2) / (2.0 * noise_level * noise_level * G * G)

def low_modes(block):
    return jnp.concatenate([block[..., :LOW // 2, :LOW], block[..., G - LOW // 2:, :LOW]], axis=-2)

def reference(particles, offspring, noise, accept, observed):
    ends = jnp.cumsum(offspring).astype(jnp.int32)
    slot_ids = jnp.arange(PARTICLES, dtype=jnp.int32)
    source = jnp.searchsorted(ends, slot_ids, side='right').astype(jnp.int32)
    present_state = jnp.take(particles, source, axis=0)
    power = lax.optimization_barrier(jnp.sum(low_modes(present_state) ** 2, axis=0)) / PARTICLES
    adapted = jnp.sqrt(power + 1e-06)
    wave_y, wave_x = wavenumbers()
    prior = prior_amplitude / (1.0 + jnp.sqrt(wave_y * wave_y + wave_x * wave_x) / 8.0)
    spread = jnp.stack([prior, prior]).astype(jnp.float32)
    spread = spread.at[:, :LOW // 2, :LOW].set(adapted[:, :LOW // 2])
    spread = spread.at[:, G - LOW // 2:, :LOW].set(adapted[:, LOW // 2:])
    keep = jnp.sqrt(1.0 - step_size * step_size)
    score_values = []
    for move in range(MOVES):
        candidate_state = keep * present_state + step_size * spread[None] * noise[move]
        score_values.append(lax.map(lambda lone_particle: predicted_state(lone_particle, observed), candidate_state))
        present_state = jnp.where(accept[move][:, None, None, None] == 1, candidate_state, present_state)
    return (present_state, jnp.stack(score_values).astype(jnp.float32))
```

```python
import functools
import math

import jax
import jax.numpy as jnp
import ml_dtypes
import numpy as np
from jax import lax
from jax.experimental import pallas as pl
from jax.experimental.pallas import tpu as pltpu
from jax.sharding import PartitionSpec as P

REACH = 3
LOW = 16
LANES = 128
COUNT_ROWS = 8
PARTS = 2
GROUP_BITS = 3

time_step = 0.05
viscosity = 0.001
noise_level = 0.5
spectral_scale = 64.0
prior_amplitude = 1.5
step_size = 0.4

MESH = pl.DeviceIdType.MESH


def split_bits(devices):
    bits = devices.bit_length() - 1
    assert 1 << bits == devices
    groups = []
    first = 0
    while first < bits:
        width = min(GROUP_BITS, bits - first)
        groups.append((first, width))
        first += width
    return groups


def exchange_kernel(
    devices, groups, x_ref, count_ref, picked_ref, total_ref,
    cand, sums, small, load_sem, big_send, big_recv, small_send, small_recv,
):
    grid = x_ref.shape[2]
    me = lax.axis_index("dom")
    core = lax.rem(me, 2)
    sibling = me + 1 - 2 * core
    left, right = me - 2, me + 2
    has_left, has_right = me >= 2, me + 2 < devices
    far = me - 3 + 6 * core
    has_far = jnp.logical_and(far >= 0, far < devices)

    load = pltpu.make_async_copy(x_ref.at[0], cand.at[REACH], load_sem)
    load.start()

    barrier = pltpu.get_barrier_semaphore()

    def greet(device):
        pl.semaphore_signal(barrier, inc=1, device_id=(device,), device_id_type=MESH)

    partners = []
    for first, width in groups:
        partners.append([jnp.bitwise_xor(me, k << first) for k in range(1, 1 << width)])
    for group in partners:
        for device in group:
            greet(device)
    pl.when(has_left)(lambda: greet(left))
    pl.when(has_right)(lambda: greet(right))
    pl.when(has_far)(lambda: greet(far))

    load.wait()
    count = count_ref[0].astype(jnp.float32)
    half_low = LOW // 2
    for part in range(PARTS):
        for at, start in enumerate((0, grid - half_low)):
            block = cand[REACH, part, start : start + half_low, :]
            row = (2 * part + at) * half_low
            sums[0, row : row + half_low, :] = block * block * count
    row_ids = lax.broadcasted_iota(jnp.int32, (COUNT_ROWS, LANES), 0)
    lane_ids = lax.broadcasted_iota(jnp.int32, (COUNT_ROWS, LANES), 1)
    order = row_ids * LANES + lane_ids
    sums[0, PARTS * LOW :, :] = jnp.where(order == me, count, 0.0)

    expected = sum(len(group) for group in partners)
    expected = expected + has_left.astype(jnp.int32) + has_right.astype(jnp.int32) + has_far.astype(jnp.int32)
    pl.semaphore_wait(barrier, expected)

    def stage_copies(stage):
        copies = []
        base = sum(len(group) for group in partners[:stage])
        for at, device in enumerate(partners[stage]):
            copies.append(
                pltpu.make_async_remote_copy(
                    src_ref=sums.at[stage],
                    dst_ref=small.at[base + at],
                    send_sem=small_send.at[base + at],
                    recv_sem=small_recv.at[base + at],
                    device_id=(device,),
                    device_id_type=MESH,
                )
            )
        return copies

    def big_copy(source, target, piece, send_at, device):
        return pltpu.make_async_remote_copy(
            src_ref=cand.at[source, piece],
            dst_ref=cand.at[target, piece],
            send_sem=big_send.at[send_at, piece],
            recv_sem=big_recv.at[target, piece],
            device_id=(device,),
            device_id_type=MESH,
        )

    own = REACH
    sends = []
    for piece in range(PARTS):
        sends.append((has_right, big_copy(own, 1, piece, 0, right)))
        sends.append((has_left, big_copy(own, 5, piece, 1, left)))
    for piece in range(PARTS):
        sends.append((has_far, big_copy(own, 6 - 6 * core, piece, 2, far)))
    for piece in range(PARTS):
        sends.append((None, big_copy(own, 2 + 2 * core, piece, 3, sibling)))
    relays = []
    for piece in range(PARTS):
        relays.append((has_left, big_copy(1, 2 * core, piece, 4, sibling), (1, piece)))
        relays.append((has_right, big_copy(5, 4 + 2 * core, piece, 5, sibling), (5, piece)))

    def arrived(slot, piece):
        big_copy(slot, slot, piece, 0, sibling).wait_recv()

    first_stage = stage_copies(0)
    for copy in first_stage:
        copy.start()
    for test, copy in sends:
        if test is None:
            copy.start()
        else:
            pl.when(test)(copy.start)

    for stage in range(len(groups)):
        copies = first_stage if stage == 0 else stage_copies(stage)
        if stage > 0:
            for copy in copies:
                copy.start()
        for copy in copies:
            copy.wait_recv()
        base = sum(len(group) for group in partners[:stage])
        total = sums[stage]
        for at in range(len(copies)):
            total = total + small[base + at]
        sums[stage + 1] = total
        for copy in copies:
            copy.wait_send()

    counts = sums[len(groups), PARTS * LOW :, :]
    total_ref[...] = sums[len(groups), : PARTS * LOW, :]
    shift = jnp.full((1, 1), -float(REACH), jnp.float32)
    slot = me.astype(jnp.float32)
    for distance in range(-REACH, REACH):
        ends = jnp.sum(jnp.where(order <= me + distance, counts, 0.0), keepdims=True)
        shift = shift + jnp.where(ends <= slot, 1.0, 0.0)

    for test, copy, (slot_at, piece) in relays:
        @pl.when(test)
        def _():
            arrived(slot_at, piece)
            copy.start()

    for piece in range(PARTS):
        arrived(4 - 2 * core, piece)

        @pl.when(has_left)
        def _():
            arrived(2 - 2 * core, piece)

        @pl.when(has_right)
        def _():
            arrived(6 - 2 * core, piece)

        @pl.when(has_far)
        def _():
            arrived(6 * core, piece)

    rows = 32
    choice = jnp.broadcast_to(shift, (rows, LANES))

    for part in range(PARTS):
        def pick(at, carry):
            span = pl.ds(pl.multiple_of(at * rows, rows), rows)
            value = cand[REACH, part, span, :]
            for distance in range(-REACH, REACH + 1):
                if distance != 0:
                    value = jnp.where(choice == distance, cand[REACH + distance, part, span, :], value)
            picked_ref[part, span, :] = value
            return carry

        lax.fori_loop(0, grid // rows, pick, 0)

    for test, copy in sends:
        if test is None:
            copy.wait_send()
        else:
            pl.when(test)(copy.wait_send)
    for test, copy, _ in relays:
        pl.when(test)(copy.wait_send)


def exchange(particles, offspring, devices):
    groups = split_bits(devices)
    _, _, grid, half = particles.shape
    assert particles.shape[0] == 1 and half == LANES and devices <= COUNT_ROWS * LANES
    copies = sum((1 << width) - 1 for _, width in groups)
    package = PARTS * LOW + COUNT_ROWS
    slots = 2 * REACH + 1
    return pl.pallas_call(
        functools.partial(exchange_kernel, devices, groups),
        out_shape=(
            jax.ShapeDtypeStruct((PARTS, grid, half), jnp.float32),
            jax.ShapeDtypeStruct((PARTS * LOW, LANES), jnp.float32),
        ),
        in_specs=[
            pl.BlockSpec(memory_space=pl.ANY),
            pl.BlockSpec(memory_space=pltpu.SMEM),
        ],
        out_specs=(
            pl.BlockSpec(memory_space=pltpu.VMEM),
            pl.BlockSpec(memory_space=pltpu.VMEM),
        ),
        scratch_shapes=[
            pltpu.VMEM((slots, PARTS, grid, half), jnp.float32),
            pltpu.VMEM((len(groups) + 1, package, LANES), jnp.float32),
            pltpu.VMEM((copies, package, LANES), jnp.float32),
            pltpu.SemaphoreType.DMA,
            pltpu.SemaphoreType.DMA((6, PARTS)),
            pltpu.SemaphoreType.DMA((slots, PARTS)),
            pltpu.SemaphoreType.DMA((copies,)),
            pltpu.SemaphoreType.DMA((copies,)),
        ],
        compiler_params=pltpu.CompilerParams(
            collective_id=0, has_side_effects=True, vmem_limit_bytes=16 * 1024 * 1024
        ),
        name="exchange",
    )(particles, offspring)


def halves(table):
    table = np.asarray(table, np.float64)
    high = table.astype(np.float32).astype(ml_dtypes.bfloat16)
    rest = (table - high.astype(np.float64)).astype(np.float32).astype(ml_dtypes.bfloat16)
    return np.stack([high, rest])


def make_tables(grid):
    half = grid // 2
    angle = 2.0 * math.pi / grid
    index = np.arange(grid)
    low = np.arange(half)
    phase = (index[:, None] * low[None, :] % grid) * angle
    sines = np.sin(phase)
    sines[:, 0] = 1.0 - 2.0 * (index % 2)
    fold = np.concatenate([np.cos(phase), sines], axis=1)
    weight = np.where(low == 0, 1.0, 2.0)[:, None]
    back = np.concatenate([weight * np.cos(phase).T, -weight * np.sin(phase).T], axis=0) / spectral_scale
    fore = np.concatenate([np.cos(phase), -np.sin(phase)], axis=1) * (spectral_scale / (grid * grid))
    flip = np.zeros((half, half))
    flip[low, (half - low) % half] = 1.0
    wave_y = np.concatenate([low, np.where(low == 0, half, low)]).astype(np.float64)[:, None]
    wave_x = low.astype(np.float64)[None, :]
    square = wave_y**2 + wave_x**2
    inverse = np.where(square > 0, 1.0 / np.maximum(square, 1.0), 0.0)
    damping = 1.0 / (1.0 + time_step * viscosity * square)
    keeper = (np.abs(wave_y) <= grid // 3) & (wave_x <= grid // 3)
    doubled = np.where(np.concatenate([low, low])[:, None] == 0, 1.0, 2.0)
    flux = -time_step * keeper * doubled * damping
    signed = np.where(index < half, index, index - grid).astype(np.float64)[:, None]
    prior = prior_amplitude / (1.0 + np.sqrt(signed**2 + wave_x**2) / 8.0)
    scales = np.stack([inverse, damping, flux, step_size * prior]).astype(np.float32)
    return (
        halves(fold), halves(fold.T), halves(back), halves(fore),
        flip.astype(ml_dtypes.bfloat16), scales,
    )


def split(value):
    high = value.astype(jnp.bfloat16)
    return high, (value - high.astype(jnp.float32)).astype(jnp.bfloat16)


def dot(a, b):
    return jnp.dot(a, b, preferred_element_type=jnp.float32)


def table_left(table, value):
    high, rest = split(value)
    return dot(table[0], high) + dot(table[0], rest) + dot(table[1], high)


def table_right(value, table):
    high, rest = split(value)
    return dot(high, table[0]) + dot(rest, table[0]) + dot(high, table[1])


def moves_kernel(
    devices, picked_ref, total_ref, noise_ref, accept_ref, observed_ref,
    fold_ref, unfold_ref, back_ref, fore_ref, flip_ref, scale_ref,
    moved_ref, misfit_ref,
):
    _, grid, half = picked_ref.shape
    moves = noise_ref.shape[0]
    half_low = LOW // 2
    keep = math.sqrt(1.0 - step_size * step_size)

    lanes = lax.broadcasted_iota(jnp.int32, (half_low, half), 1)

    def spread(part):
        prior = scale_ref[3]
        top, bottom = prior[:half_low], prior[grid - half_low :]
        total = total_ref[part * LOW : (part + 1) * LOW, :]
        adapted = step_size * jnp.sqrt(total * (1.0 / devices) + 1e-06)
        top = jnp.where(lanes < LOW, adapted[:half_low], top)
        bottom = jnp.where(lanes < LOW, adapted[half_low:], bottom)
        return jnp.concatenate([top, prior[half_low : grid - half_low], bottom], axis=0)

    spreads = [spread(part) for part in range(PARTS)]
    present = [picked_ref[part] for part in range(PARTS)]
    proposals = []
    for move in range(moves):
        taken = accept_ref[move, 0] == 1
        candidate = [keep * present[part] + spreads[part] * noise_ref[move, 0, part] for part in range(PARTS)]
        present = [jnp.where(taken, candidate[part], present[part]) for part in range(PARTS)]
        proposals.append(candidate)
    for part in range(PARTS):
        moved_ref[0, part] = present[part]

    row_ids = lax.broadcasted_iota(jnp.int32, (half, grid), 0)
    first = row_ids == 0
    wave = row_ids.astype(jnp.float32)
    wave_x = lax.broadcasted_iota(jnp.int32, (grid, half), 1).astype(jnp.float32)
    fold = (fold_ref[0], fold_ref[1])
    unfold = (unfold_ref[0], unfold_ref[1])
    back = (back_ref[0], back_ref[1])
    fore = (fore_ref[0], fore_ref[1])
    flip = flip_ref[...]

    def wide(index):
        value = scale_ref[index]
        return jnp.concatenate([value, value], axis=1)

    def turn(value):
        return jnp.concatenate([-value[:, half:], value[:, :half]], axis=1)

    states = []
    for real_part, imag_part in proposals:
        top = jnp.concatenate([real_part[:half], imag_part[:half]], axis=1)
        high, rest = split(jnp.concatenate([real_part[half:], imag_part[half:]], axis=1))
        other = dot(flip, high) + dot(flip, rest)
        even = top + jnp.where(first, 0.0, other)
        odd = jnp.where(first, other, turn(top - other))
        states.append(jnp.concatenate([even, odd], axis=0))

    inverse = wide(0)
    rows = []
    for state in states:
        psi = state * inverse
        psi_even, psi_odd = psi[:half], psi[half:]
        along_y = jnp.concatenate(
            [wave * psi_odd, jnp.where(first, -float(half) * turn(psi_odd), -wave * psi_even)], axis=0
        )
        along_x = jnp.concatenate([wave_x * psi[:, half:], -wave_x * psi[:, :half]], axis=1)
        for value in (state, along_y, along_x):
            rows.append(table_left(fold, value))
    fields = table_right(jnp.concatenate(rows, axis=0), back)

    products = []
    for move in range(moves):
        vort = fields[(3 * move) * grid : (3 * move + 1) * grid]
        for at in (1, 2):
            products.append(fields[(3 * move + at) * grid : (3 * move + at + 1) * grid] * vort)
    flux_rows = table_right(jnp.concatenate(products, axis=0), fore)

    damping = wide(1)
    flux_scale = wide(2)
    finals = []
    for move in range(moves):
        flux_u = table_left(unfold, flux_rows[(2 * move) * grid : (2 * move + 1) * grid])
        flux_v = table_left(unfold, flux_rows[(2 * move + 1) * grid : (2 * move + 2) * grid])
        along_x = jnp.concatenate([-wave_x * flux_u[:, half:], wave_x * flux_u[:, :half]], axis=1)
        along_y = jnp.concatenate([wave * flux_v[half:], -wave * flux_v[:half]], axis=0)
        state = states[move] * damping + flux_scale * (along_x + along_y)
        finals.append(table_left(fold, state))
    forecast = table_right(jnp.concatenate(finals, axis=0), back)
    for move in range(moves):
        gap = forecast[move * grid : (move + 1) * grid] - observed_ref[...]
        misfit_ref[move, 0] = jnp.sum(gap * gap) * (1.0 / (2.0 * noise_level * noise_level * grid * grid))


def apply_moves(picked, totals, noise, accept, observed, devices):
    _, grid, half = picked.shape
    moves = noise.shape[0]
    tables = [jnp.asarray(table) for table in make_tables(grid)]
    flops = 2 * moves * 36 * grid**3
    vmem = pl.BlockSpec(memory_space=pltpu.VMEM)
    smem = pl.BlockSpec(memory_space=pltpu.SMEM)
    return pl.pallas_call(
        functools.partial(moves_kernel, devices),
        out_shape=(
            jax.ShapeDtypeStruct((1, PARTS, grid, half), jnp.float32),
            jax.ShapeDtypeStruct((moves, 1), jnp.float32),
        ),
        in_specs=[vmem, vmem, vmem, smem] + [vmem] * 7,
        out_specs=(vmem, smem),
        cost_estimate=pl.CostEstimate(flops=flops, bytes_accessed=4 * 1024 * 1024, transcendentals=0),
        compiler_params=pltpu.CompilerParams(vmem_limit_bytes=40 * 1024 * 1024),
        name="moves",
    )(picked, totals, noise, accept, observed, *tables)


def body(devices, particles, offspring, noise, accept, observed):
    picked, totals = exchange(particles, offspring, devices)
    return apply_moves(picked, totals, noise, accept, observed, devices)


def solution(mesh):
    return jax.shard_map(
        functools.partial(body, mesh.shape["dom"]),
        mesh=mesh,
        in_specs=(
            P("dom", None, None, None),
            P("dom"),
            P(None, "dom", None, None, None),
            P(None, "dom"),
            P(),
        ),
        out_specs=(P("dom", None, None, None), P(None, "dom")),
        check_vma=False,
    )
```

```python
import functools
import math

import jax
import jax.numpy as jnp
import ml_dtypes
import numpy as np
from jax import lax
from jax.experimental import pallas as pl
from jax.experimental.pallas import tpu as pltpu
from jax.sharding import PartitionSpec as P

REACH = 3
LOW = 16
LANES = 128
COUNT_ROWS = 8
PARTS = 2
GROUP_BITS = 3

time_step = 0.05
viscosity = 0.001
noise_level = 0.5
spectral_scale = 64.0
prior_amplitude = 1.5
step_size = 0.4

MESH = pl.DeviceIdType.MESH
HBM = pltpu.MemorySpace.HBM


def split_bits(devices):
    bits = devices.bit_length() - 1
    assert 1 << bits == devices
    groups = []
    first = 0
    while first < bits:
        width = min(GROUP_BITS, bits - first)
        groups.append((first, width))
        first += width
    return groups


def filter_kernel(
    devices, groups, x_ref, count_ref, accept_ref, noise_hbm, observed_hbm, *rest
):
    tables_hbm = rest[:6]
    moved_ref, misfit_ref = rest[6:8]
    cand, sums, small, picked_ref, noise_ref, observed_ref = rest[8:14]
    tables = rest[14:20]
    load_sem, big_send, big_recv, small_send, small_recv, fetch_sem = rest[20:]
    grid = x_ref.shape[2]
    me = lax.axis_index("dom")
    core = lax.rem(me, 2)
    sibling = me + 1 - 2 * core
    left, right = me - 2, me + 2
    has_left, has_right = me >= 2, me + 2 < devices
    far = me - 3 + 6 * core
    has_far = jnp.logical_and(far >= 0, far < devices)

    load = pltpu.make_async_copy(x_ref.at[0], cand.at[REACH], load_sem)
    load.start()
    fetches = [
        pltpu.make_async_copy(source, target, fetch_sem.at[at])
        for at, (source, target) in enumerate(
            zip((noise_hbm, observed_hbm) + tables_hbm, (noise_ref, observed_ref) + tables)
        )
    ]
    for fetch in fetches:
        fetch.start()

    barrier = pltpu.get_barrier_semaphore()

    def greet(device):
        pl.semaphore_signal(barrier, inc=1, device_id=(device,), device_id_type=MESH)

    partners = []
    for first, width in groups:
        partners.append([jnp.bitwise_xor(me, k << first) for k in range(1, 1 << width)])
    for group in partners:
        for device in group:
            greet(device)
    pl.when(has_left)(lambda: greet(left))
    pl.when(has_right)(lambda: greet(right))
    pl.when(has_far)(lambda: greet(far))

    load.wait()
    count = count_ref[0].astype(jnp.float32)
    half_low = LOW // 2
    for part in range(PARTS):
        for at, start in enumerate((0, grid - half_low)):
            block = cand[REACH, part, start : start + half_low, :]
            row = (2 * part + at) * half_low
            sums[0, row : row + half_low, :] = block * block * count
    row_ids = lax.broadcasted_iota(jnp.int32, (COUNT_ROWS, LANES), 0)
    lane_ids = lax.broadcasted_iota(jnp.int32, (COUNT_ROWS, LANES), 1)
    order = row_ids * LANES + lane_ids
    sums[0, PARTS * LOW :, :] = jnp.where(order == me, count, 0.0)

    expected = sum(len(group) for group in partners)
    expected = expected + has_left.astype(jnp.int32) + has_right.astype(jnp.int32) + has_far.astype(jnp.int32)
    pl.semaphore_wait(barrier, expected)

    def stage_copies(stage):
        copies = []
        base = sum(len(group) for group in partners[:stage])
        for at, device in enumerate(partners[stage]):
            copies.append(
                pltpu.make_async_remote_copy(
                    src_ref=sums.at[stage],
                    dst_ref=small.at[base + at],
                    send_sem=small_send.at[base + at],
                    recv_sem=small_recv.at[base + at],
                    device_id=(device,),
                    device_id_type=MESH,
                )
            )
        return copies

    def big_copy(source, target, piece, send_at, device):
        return pltpu.make_async_remote_copy(
            src_ref=cand.at[source, piece],
            dst_ref=cand.at[target, piece],
            send_sem=big_send.at[send_at, piece],
            recv_sem=big_recv.at[target, piece],
            device_id=(device,),
            device_id_type=MESH,
        )

    own = REACH
    sends = []
    for piece in range(PARTS):
        sends.append((has_right, big_copy(own, 1, piece, 0, right)))
        sends.append((has_left, big_copy(own, 5, piece, 1, left)))
    for piece in range(PARTS):
        sends.append((has_far, big_copy(own, 6 - 6 * core, piece, 2, far)))
    for piece in range(PARTS):
        sends.append((None, big_copy(own, 2 + 2 * core, piece, 3, sibling)))
    relays = []
    for piece in range(PARTS):
        relays.append((has_left, big_copy(1, 2 * core, piece, 4, sibling), (1, piece)))
        relays.append((has_right, big_copy(5, 4 + 2 * core, piece, 5, sibling), (5, piece)))

    def arrived(slot, piece):
        big_copy(slot, slot, piece, 0, sibling).wait_recv()

    first_stage = stage_copies(0)
    for copy in first_stage:
        copy.start()
    for test, copy in sends:
        if test is None:
            copy.start()
        else:
            pl.when(test)(copy.start)

    for stage in range(len(groups)):
        copies = first_stage if stage == 0 else stage_copies(stage)
        if stage > 0:
            for copy in copies:
                copy.start()
        for copy in copies:
            copy.wait_recv()
        base = sum(len(group) for group in partners[:stage])
        total = sums[stage]
        for at in range(len(copies)):
            total = total + small[base + at]
        sums[stage + 1] = total
        for copy in copies:
            copy.wait_send()

    counts = sums[len(groups), PARTS * LOW :, :]
    shift = jnp.full((1, 1), -float(REACH), jnp.float32)
    slot = me.astype(jnp.float32)
    for distance in range(-REACH, REACH):
        ends = jnp.sum(jnp.where(order <= me + distance, counts, 0.0), keepdims=True)
        shift = shift + jnp.where(ends <= slot, 1.0, 0.0)

    for test, copy, (slot_at, piece) in relays:
        @pl.when(test)
        def _():
            arrived(slot_at, piece)
            copy.start()

    for fetch in fetches:
        fetch.wait()
    work = Work(devices, grid, tables)
    totals = sums[len(groups), : PARTS * LOW, :]
    drift = work.drifts(noise_ref, totals)
    taken = [accept_ref[0, move] == 1 for move in range(len(drift))]
    gains, offsets = work.unrolled(drift, taken)
    offset_states = [work.folded(value) for value in offsets]
    offset_fields = [work.fields(state) for state in offset_states]

    for piece in range(PARTS):
        arrived(4 - 2 * core, piece)

        @pl.when(has_left)
        def _():
            arrived(2 - 2 * core, piece)

        @pl.when(has_right)
        def _():
            arrived(6 - 2 * core, piece)

        @pl.when(has_far)
        def _():
            arrived(6 * core, piece)

    rows = 32
    choice = jnp.broadcast_to(shift, (rows, LANES))

    for part in range(PARTS):
        def pick(at, carry):
            span = pl.ds(pl.multiple_of(at * rows, rows), rows)
            value = cand[REACH, part, span, :]
            for distance in range(-REACH, REACH + 1):
                if distance != 0:
                    value = jnp.where(choice == distance, cand[REACH + distance, part, span, :], value)
            picked_ref[part, span, :] = value
            return carry

        lax.fori_loop(0, grid // rows, pick, 0)

    for test, copy in sends:
        if test is None:
            copy.wait_send()
        else:
            pl.when(test)(copy.wait_send)
    for test, copy, _ in relays:
        pl.when(test)(copy.wait_send)

    present = [picked_ref[part] for part in range(PARTS)]
    moved = present
    for move in range(len(drift)):
        candidate = [work.keep * moved[part] + drift[move][part] for part in range(PARTS)]
        moved = [jnp.where(taken[move], candidate[part], moved[part]) for part in range(PARTS)]
    for part in range(PARTS):
        moved_ref[0, part] = moved[part]

    base_state = work.folded(present)
    base_fields = work.fields(base_state)
    states = [gain * base_state + state for gain, state in zip(gains, offset_states)]
    fields = [gain * base_fields + value for gain, value in zip(gains, offset_fields)]
    for move, score in enumerate(work.scores(states, fields, observed_ref)):
        misfit_ref[0, move] = score


def halves(table):
    table = np.asarray(table, np.float64)
    high = table.astype(np.float32).astype(ml_dtypes.bfloat16)
    rest = (table - high.astype(np.float64)).astype(np.float32).astype(ml_dtypes.bfloat16)
    return np.stack([high, rest])


def make_tables(grid):
    half = grid // 2
    angle = 2.0 * math.pi / grid
    index = np.arange(grid)
    low = np.arange(half)
    phase = (index[:, None] * low[None, :] % grid) * angle
    sines = np.sin(phase)
    sines[:, 0] = 1.0 - 2.0 * (index % 2)
    fold = np.concatenate([np.cos(phase), sines], axis=1)
    weight = np.where(low == 0, 1.0, 2.0)[:, None]
    back = np.concatenate([weight * np.cos(phase).T, -weight * np.sin(phase).T], axis=0) / spectral_scale
    fore = np.concatenate([np.cos(phase), -np.sin(phase)], axis=1) * (spectral_scale / (grid * grid))
    flip = np.zeros((half, half))
    flip[low, (half - low) % half] = 1.0
    wave_y = np.concatenate([low, np.where(low == 0, half, low)]).astype(np.float64)[:, None]
    wave_x = low.astype(np.float64)[None, :]
    square = wave_y**2 + wave_x**2
    inverse = np.where(square > 0, 1.0 / np.maximum(square, 1.0), 0.0)
    damping = 1.0 / (1.0 + time_step * viscosity * square)
    keeper = (np.abs(wave_y) <= grid // 3) & (wave_x <= grid // 3)
    doubled = np.where(np.concatenate([low, low])[:, None] == 0, 1.0, 2.0)
    flux = -time_step * keeper * doubled * damping
    signed = np.where(index < half, index, index - grid).astype(np.float64)[:, None]
    prior = prior_amplitude / (1.0 + np.sqrt(signed**2 + wave_x**2) / 8.0)
    scales = np.stack([inverse, damping, flux, step_size * prior]).astype(np.float32)
    return (
        halves(fold), halves(fold.T), halves(back), halves(fore),
        flip.astype(ml_dtypes.bfloat16), scales,
    )


def split(value):
    high = value.astype(jnp.bfloat16)
    return high, (value - high.astype(jnp.float32)).astype(jnp.bfloat16)


def dot(a, b):
    return jnp.dot(a, b, preferred_element_type=jnp.float32)


def table_left(table, value):
    high, rest = split(value)
    return dot(table[0], high) + dot(table[0], rest) + dot(table[1], high)


def table_right(value, table):
    high, rest = split(value)
    return dot(high, table[0]) + dot(rest, table[0]) + dot(high, table[1])


class Work:
    def __init__(self, devices, grid, tables):
        fold, unfold, back, fore, flip, scales = tables
        self.devices, self.grid, self.half = devices, grid, grid // 2
        self.fold = (fold[0], fold[1])
        self.unfold = (unfold[0], unfold[1])
        self.back = (back[0], back[1])
        self.fore = (fore[0], fore[1])
        self.flip = flip[...]
        self.scales = scales
        self.keep = math.sqrt(1.0 - step_size * step_size)
        row_ids = lax.broadcasted_iota(jnp.int32, (self.half, grid), 0)
        self.first = row_ids == 0
        self.wave = row_ids.astype(jnp.float32)
        self.wave_x = lax.broadcasted_iota(jnp.int32, (grid, self.half), 1).astype(jnp.float32)

    def wide(self, index):
        value = self.scales[index]
        return jnp.concatenate([value, value], axis=1)

    def turn(self, value):
        return jnp.concatenate([-value[:, self.half :], value[:, : self.half]], axis=1)

    def drifts(self, noise_ref, totals):
        half_low = LOW // 2
        lanes = lax.broadcasted_iota(jnp.int32, (half_low, self.half), 1)
        prior = self.scales[3]
        inner = slice(half_low, self.grid - half_low)
        spreads = []
        for part in range(PARTS):
            total = totals[part * LOW : (part + 1) * LOW, :]
            adapted = step_size * jnp.sqrt(total * (1.0 / self.devices) + 1e-06)
            top = jnp.where(lanes < LOW, adapted[:half_low], prior[:half_low])
            bottom = jnp.where(lanes < LOW, adapted[half_low:], prior[self.grid - half_low :])
            spreads.append(jnp.concatenate([top, prior[inner], bottom], axis=0))
        return [
            [spreads[part] * noise_ref[move, 0, part] for part in range(PARTS)]
            for move in range(noise_ref.shape[0])
        ]

    def unrolled(self, drift, taken):
        gain, offset = 1.0, [jnp.zeros_like(value) for value in drift[0]]
        gains, offsets = [], []
        for step, accepted in zip(drift, taken):
            new_gain = self.keep * gain
            new_offset = [self.keep * old + value for old, value in zip(offset, step)]
            gains.append(new_gain)
            offsets.append(new_offset)
            gain = jnp.where(accepted, new_gain, gain)
            offset = [jnp.where(accepted, new, old) for new, old in zip(new_offset, offset)]
        return gains, offsets

    def folded(self, parts):
        half = self.half
        top = jnp.concatenate([part[:half] for part in parts], axis=1)
        high, rest = split(jnp.concatenate([part[half:] for part in parts], axis=1))
        other = dot(self.flip, high) + dot(self.flip, rest)
        even = top + jnp.where(self.first, 0.0, other)
        odd = jnp.where(self.first, other, self.turn(top - other))
        return jnp.concatenate([even, odd], axis=0)

    def fields(self, state):
        half, wave_x = self.half, self.wave_x
        psi = state * self.wide(0)
        even, odd = psi[:half], psi[half:]
        along_y = jnp.concatenate(
            [self.wave * odd, jnp.where(self.first, -float(half) * self.turn(odd), -self.wave * even)], axis=0
        )
        along_x = jnp.concatenate([wave_x * psi[:, half:], -wave_x * psi[:, :half]], axis=1)
        rows = [table_left(self.fold, value) for value in (state, along_y, along_x)]
        return table_right(jnp.concatenate(rows, axis=0), self.back)

    def scores(self, states, fields, observed_ref):
        grid, half, wave, wave_x = self.grid, self.half, self.wave, self.wave_x
        products = []
        for value in fields:
            vort = value[:grid]
            products += [value[grid : 2 * grid] * vort, value[2 * grid :] * vort]
        rows = table_right(jnp.concatenate(products, axis=0), self.fore)
        damping, flux_scale = self.wide(1), self.wide(2)
        finals = []
        for move, state in enumerate(states):
            flux_u = table_left(self.unfold, rows[(2 * move) * grid : (2 * move + 1) * grid])
            flux_v = table_left(self.unfold, rows[(2 * move + 1) * grid : (2 * move + 2) * grid])
            along_x = jnp.concatenate([-wave_x * flux_u[:, half:], wave_x * flux_u[:, :half]], axis=1)
            along_y = jnp.concatenate([wave * flux_v[half:], -wave * flux_v[:half]], axis=0)
            finals.append(table_left(self.fold, state * damping + flux_scale * (along_x + along_y)))
        forecast = table_right(jnp.concatenate(finals, axis=0), self.back)
        scale = 1.0 / (2.0 * noise_level * noise_level * grid * grid)
        result = []
        for move in range(len(states)):
            gap = forecast[move * grid : (move + 1) * grid] - observed_ref[...]
            result.append(jnp.sum(gap * gap) * scale)
        return result


def body(devices, particles, offspring, noise, accept, observed):
    groups = split_bits(devices)
    _, _, grid, half = particles.shape
    moves = noise.shape[0]
    assert particles.shape[0] == 1 and half == LANES and devices <= COUNT_ROWS * LANES
    copies = sum((1 << width) - 1 for _, width in groups)
    package = PARTS * LOW + COUNT_ROWS
    slots = 2 * REACH + 1
    tables = [jnp.asarray(table) for table in make_tables(grid)]
    hbm = pl.BlockSpec(memory_space=HBM)
    smem = pl.BlockSpec(memory_space=pltpu.SMEM)
    fetched = [noise, observed] + tables
    moved, misfit = pl.pallas_call(
        functools.partial(filter_kernel, devices, groups),
        out_shape=(
            jax.ShapeDtypeStruct((1, PARTS, grid, half), jnp.float32),
            jax.ShapeDtypeStruct((1, moves), jnp.float32),
        ),
        in_specs=[hbm, smem, smem] + [hbm] * len(fetched),
        out_specs=(pl.BlockSpec(memory_space=pltpu.VMEM), smem),
        scratch_shapes=[
            pltpu.VMEM((slots, PARTS, grid, half), jnp.float32),
            pltpu.VMEM((len(groups) + 1, package, LANES), jnp.float32),
            pltpu.VMEM((copies, package, LANES), jnp.float32),
            pltpu.VMEM((PARTS, grid, half), jnp.float32),
        ]
        + [pltpu.VMEM(value.shape, value.dtype) for value in fetched]
        + [
            pltpu.SemaphoreType.DMA,
            pltpu.SemaphoreType.DMA((6, PARTS)),
            pltpu.SemaphoreType.DMA((slots, PARTS)),
            pltpu.SemaphoreType.DMA((copies,)),
            pltpu.SemaphoreType.DMA((copies,)),
            pltpu.SemaphoreType.DMA((len(fetched),)),
        ],
        compiler_params=pltpu.CompilerParams(
            collective_id=0, has_side_effects=True, vmem_limit_bytes=63 * 1024 * 1024
        ),
        name="filter",
    )(particles, offspring, accept.T, *fetched)
    return moved, misfit.T


def solution(mesh):
    return jax.shard_map(
        functools.partial(body, mesh.shape["dom"]),
        mesh=mesh,
        in_specs=(
            P("dom", None, None, None),
            P("dom"),
            P(None, "dom", None, None, None),
            P(None, "dom"),
            P(),
        ),
        out_specs=(P("dom", None, None, None), P(None, "dom")),
        check_vma=False,
    )
```

```python
import functools
import math

import jax
import jax.numpy as jnp
import ml_dtypes
import numpy as np
from jax import lax
from jax.experimental import pallas as pl
from jax.experimental.pallas import tpu as pltpu
from jax.sharding import PartitionSpec as P

REACH = 3
LOW = 16
LANES = 128
COUNT_ROWS = 8
PARTS = 2
GROUP_BITS = 3
TEAM = 4
CHUNKS = 4

time_step = 0.05
viscosity = 0.001
noise_level = 0.5
spectral_scale = 64.0
prior_amplitude = 1.5
step_size = 0.4

MESH = pl.DeviceIdType.MESH
HBM = pltpu.MemorySpace.HBM


def split_bits(devices):
    bits = devices.bit_length() - 1
    assert 1 << bits == devices
    groups = []
    first = 0
    while first < bits:
        width = min(GROUP_BITS, bits - first)
        groups.append((first, width))
        first += width
    return groups


def filter_kernel(
    devices, groups, x_ref, count_ref, accept_ref, noise_hbm, observed_hbm, *rest
):
    tables_hbm = rest[:6]
    moved_ref, misfit_ref = rest[6:8]
    cand, chosen, sums, small, noise_ref, observed_ref = rest[8:14]
    tables = rest[14:20]
    load_sem, whole_sem, cross_sem, relay_sem, chosen_sem, small_send, small_recv, fetch_sem = rest[20:]
    chunks, chunk_rows, _ = x_ref.shape
    grid = chunks * chunk_rows // PARTS
    me = lax.axis_index("dom")
    place = lax.rem(me, TEAM)
    start = me - place
    core = lax.rem(place, 2)
    side = place // 2
    near = place + 1 - 2 * core
    across = lax.rem(place + 2, TEAM)
    both = lax.rem(near + 2, TEAM)
    sibling, partner = start + near, start + across
    chosen_to = me + TEAM - 2 * TEAM * side
    chosen_from = me - TEAM + 2 * TEAM * side
    sends_chosen = jnp.logical_and(chosen_to >= 0, chosen_to < devices)
    takes_chosen = jnp.logical_and(chosen_from >= 0, chosen_from < devices)
    far_to = jnp.where(place == 0, me - REACH, me + REACH)
    far_from = jnp.where(place == 1, me + REACH, me - REACH)
    outer = jnp.logical_or(place == 0, place == TEAM - 1)
    sends_far = jnp.logical_and(outer, jnp.logical_and(far_to >= 0, far_to < devices))
    takes_far = jnp.logical_and(
        jnp.logical_not(outer), jnp.logical_and(far_from >= 0, far_from < devices)
    )

    load = pltpu.make_async_copy(x_ref, cand.at[place], load_sem)
    load.start()
    fetches = [
        pltpu.make_async_copy(source, target, fetch_sem.at[at])
        for at, (source, target) in enumerate(
            zip((noise_hbm, observed_hbm) + tables_hbm, (noise_ref, observed_ref) + tables)
        )
    ]
    for fetch in fetches:
        fetch.start()

    barrier = pltpu.get_barrier_semaphore()

    def greet(device):
        pl.semaphore_signal(barrier, inc=1, device_id=(device,), device_id_type=MESH)

    partners = []
    for first, width in groups:
        partners.append([jnp.bitwise_xor(me, k << first) for k in range(1, 1 << width)])
    for group in partners:
        for device in group:
            greet(device)
    pl.when(takes_chosen)(lambda: greet(chosen_from))
    pl.when(takes_far)(lambda: greet(far_from))

    load.wait()
    count = count_ref[0].astype(jnp.float32)
    half_low = LOW // 2
    per_part = chunks // PARTS
    for part in range(PARTS):
        ends = (
            cand[place, part * per_part, :half_low, :],
            cand[place, (part + 1) * per_part - 1, chunk_rows - half_low :, :],
        )
        for at, block in enumerate(ends):
            row = (2 * part + at) * half_low
            sums[0, row : row + half_low, :] = block * block * count
    row_ids = lax.broadcasted_iota(jnp.int32, (COUNT_ROWS, LANES), 0)
    lane_ids = lax.broadcasted_iota(jnp.int32, (COUNT_ROWS, LANES), 1)
    order = row_ids * LANES + lane_ids
    sums[0, PARTS * LOW :, :] = jnp.where(order == me, count, 0.0)

    expected = sum(len(group) for group in partners)
    pl.semaphore_wait(barrier, expected + sends_chosen.astype(jnp.int32) + sends_far.astype(jnp.int32))

    def remote(source, target, pair, device):
        return pltpu.make_async_remote_copy(
            src_ref=source,
            dst_ref=target,
            send_sem=pair.at[0],
            recv_sem=pair.at[1],
            device_id=(device,),
            device_id_type=MESH,
        )

    def stage_copies(stage):
        copies = []
        base = sum(len(group) for group in partners[:stage])
        for at, device in enumerate(partners[stage]):
            copies.append(
                pltpu.make_async_remote_copy(
                    src_ref=sums.at[stage],
                    dst_ref=small.at[base + at],
                    send_sem=small_send.at[base + at],
                    recv_sem=small_recv.at[base + at],
                    device_id=(device,),
                    device_id_type=MESH,
                )
            )
        return copies

    def cross(slot, chunk):
        return remote(cand.at[slot, chunk], cand.at[slot, chunk], cross_sem.at[chunk], partner)

    def relay(slot, chunk):
        return remote(cand.at[slot, chunk], cand.at[slot, chunk], relay_sem.at[chunk], sibling)

    def forward(chunk):
        return remote(chosen.at[chunk], cand.at[TEAM, chunk], chosen_sem.at[chunk], chosen_to)

    to_sibling = remote(cand.at[place], cand.at[place], whole_sem.at[0], sibling)
    from_sibling = remote(cand.at[near], cand.at[near], whole_sem.at[0], sibling)
    to_far = remote(cand.at[place], cand.at[TEAM + 1], whole_sem.at[1], far_to)

    first_stage = stage_copies(0)
    for copy in first_stage:
        copy.start()
    for chunk in range(chunks):
        cross(place, chunk).start()
    to_sibling.start()
    pl.when(sends_far)(to_far.start)

    for stage in range(len(groups)):
        copies = first_stage if stage == 0 else stage_copies(stage)
        if stage > 0:
            for copy in copies:
                copy.start()
        for copy in copies:
            copy.wait_recv()
        base = sum(len(group) for group in partners[:stage])
        total = sums[stage]
        for at in range(len(copies)):
            total = total + small[base + at]
        sums[stage + 1] = total
        for copy in copies:
            copy.wait_send()

    counts = sums[len(groups), PARTS * LOW :, :]

    def source_place(slot):
        found = jnp.full((1, 1), 1.0, jnp.float32) * (slot - REACH - start).astype(jnp.float32)
        for distance in range(-REACH, REACH):
            ends = jnp.sum(jnp.where(order <= slot + distance, counts, 0.0), keepdims=True)
            found = found + jnp.where(ends <= slot.astype(jnp.float32), 1.0, 0.0)
        return jnp.broadcast_to(found, (chunk_rows, LANES))

    forward_place = source_place(chosen_to)
    from_sibling.wait_recv()

    def team_value(which, chunk):
        value = cand[0, chunk]
        for at in range(1, TEAM):
            value = jnp.where(which == at, cand[at, chunk], value)
        return value

    def pass_on(chunk):
        cross(across, chunk).wait_recv()
        relay(across, chunk).start()

    def send_chosen(chunk):
        relay(both, chunk).wait_recv()
        chosen[chunk] = team_value(forward_place, chunk)
        pl.when(sends_chosen)(forward(chunk).start)

    pass_on(0)
    for chunk in range(1, chunks):
        pass_on(chunk)
        send_chosen(chunk - 1)
    send_chosen(chunks - 1)

    for fetch in fetches:
        fetch.wait()
    work = Work(devices, grid, tables)
    totals = sums[len(groups), : PARTS * LOW, :]
    drift = work.drifts(noise_ref, totals)
    taken = [accept_ref[0, move] == 1 for move in range(len(drift))]
    gains, offsets = work.unrolled(drift, taken)
    offset_states = [work.folded(value) for value in offsets]
    offset_fields = [work.fields(state) for state in offset_states]

    own_place = source_place(me)
    first_side = jnp.broadcast_to(jnp.full((1, 1), 1.0, jnp.float32) * side.astype(jnp.float32), (chunk_rows, LANES)) < 0.5
    before, after = own_place < 0.0, own_place > TEAM - 1.0
    use_chosen = jnp.logical_or(jnp.logical_and(first_side, before), jnp.logical_and(jnp.logical_not(first_side), after))
    use_far = jnp.logical_and(jnp.logical_or(before, after), jnp.logical_not(use_chosen))

    def arrived_far():
        remote(cand.at[TEAM + 1], cand.at[TEAM + 1], whole_sem.at[1], far_from).wait_recv()

    pl.when(takes_far)(arrived_far)
    pieces = []
    for chunk in range(chunks):
        def arrived():
            remote(chosen.at[chunk], cand.at[TEAM, chunk], chosen_sem.at[chunk], chosen_from).wait_recv()

        pl.when(takes_chosen)(arrived)
        value = team_value(own_place, chunk)
        value = jnp.where(use_chosen, cand[TEAM, chunk], value)
        pieces.append(jnp.where(use_far, cand[TEAM + 1, chunk], value))
    present = [jnp.concatenate(pieces[part * per_part : (part + 1) * per_part], axis=0) for part in range(PARTS)]

    moved = present
    for move in range(len(drift)):
        candidate = [work.keep * moved[part] + drift[move][part] for part in range(PARTS)]
        moved = [jnp.where(taken[move], candidate[part], moved[part]) for part in range(PARTS)]
    for part in range(PARTS):
        moved_ref[0, part] = moved[part]

    base_state = work.folded(present)
    base_fields = work.fields(base_state)
    states = [gain * base_state + state for gain, state in zip(gains, offset_states)]
    fields = [gain * base_fields + value for gain, value in zip(gains, offset_fields)]
    for move, score in enumerate(work.scores(states, fields, observed_ref)):
        misfit_ref[0, move] = score

    to_sibling.wait_send()
    pl.when(sends_far)(to_far.wait_send)
    for chunk in range(chunks):
        cross(place, chunk).wait_send()
        relay(across, chunk).wait_send()
        pl.when(sends_chosen)(forward(chunk).wait_send)


def halves(table):
    table = np.asarray(table, np.float64)
    high = table.astype(np.float32).astype(ml_dtypes.bfloat16)
    rest = (table - high.astype(np.float64)).astype(np.float32).astype(ml_dtypes.bfloat16)
    return np.stack([high, rest])


def make_tables(grid):
    half = grid // 2
    angle = 2.0 * math.pi / grid
    index = np.arange(grid)
    low = np.arange(half)
    phase = (index[:, None] * low[None, :] % grid) * angle
    sines = np.sin(phase)
    sines[:, 0] = 1.0 - 2.0 * (index % 2)
    fold = np.concatenate([np.cos(phase), sines], axis=1)
    weight = np.where(low == 0, 1.0, 2.0)[:, None]
    back = np.concatenate([weight * np.cos(phase).T, -weight * np.sin(phase).T], axis=0) / spectral_scale
    fore = np.concatenate([np.cos(phase), -np.sin(phase)], axis=1) * (spectral_scale / (grid * grid))
    flip = np.zeros((half, half))
    flip[low, (half - low) % half] = 1.0
    wave_y = np.concatenate([low, np.where(low == 0, half, low)]).astype(np.float64)[:, None]
    wave_x = low.astype(np.float64)[None, :]
    square = wave_y**2 + wave_x**2
    inverse = np.where(square > 0, 1.0 / np.maximum(square, 1.0), 0.0)
    damping = 1.0 / (1.0 + time_step * viscosity * square)
    keeper = (np.abs(wave_y) <= grid // 3) & (wave_x <= grid // 3)
    doubled = np.where(np.concatenate([low, low])[:, None] == 0, 1.0, 2.0)
    flux = -time_step * keeper * doubled * damping
    signed = np.where(index < half, index, index - grid).astype(np.float64)[:, None]
    prior = prior_amplitude / (1.0 + np.sqrt(signed**2 + wave_x**2) / 8.0)
    scales = np.stack([inverse, damping, flux, step_size * prior]).astype(np.float32)
    return (
        halves(fold), halves(fold.T), halves(back), halves(fore),
        flip.astype(ml_dtypes.bfloat16), scales,
    )


def split(value):
    high = value.astype(jnp.bfloat16)
    return high, (value - high.astype(jnp.float32)).astype(jnp.bfloat16)


def dot(a, b):
    return jnp.dot(a, b, preferred_element_type=jnp.float32)


def table_left(table, value):
    high, rest = split(value)
    return dot(table[0], high) + dot(table[0], rest) + dot(table[1], high)


def table_right(value, table):
    high, rest = split(value)
    return dot(high, table[0]) + dot(rest, table[0]) + dot(high, table[1])


class Work:
    def __init__(self, devices, grid, tables):
        fold, unfold, back, fore, flip, scales = tables
        self.devices, self.grid, self.half = devices, grid, grid // 2
        self.fold = (fold[0], fold[1])
        self.unfold = (unfold[0], unfold[1])
        self.back = (back[0], back[1])
        self.fore = (fore[0], fore[1])
        self.flip = flip[...]
        self.scales = scales
        self.keep = math.sqrt(1.0 - step_size * step_size)
        row_ids = lax.broadcasted_iota(jnp.int32, (self.half, grid), 0)
        self.first = row_ids == 0
        self.wave = row_ids.astype(jnp.float32)
        self.wave_x = lax.broadcasted_iota(jnp.int32, (grid, self.half), 1).astype(jnp.float32)

    def wide(self, index):
        value = self.scales[index]
        return jnp.concatenate([value, value], axis=1)

    def turn(self, value):
        return jnp.concatenate([-value[:, self.half :], value[:, : self.half]], axis=1)

    def drifts(self, noise_ref, totals):
        half_low = LOW // 2
        lanes = lax.broadcasted_iota(jnp.int32, (half_low, self.half), 1)
        prior = self.scales[3]
        inner = slice(half_low, self.grid - half_low)
        spreads = []
        for part in range(PARTS):
            total = totals[part * LOW : (part + 1) * LOW, :]
            adapted = step_size * jnp.sqrt(total * (1.0 / self.devices) + 1e-06)
            top = jnp.where(lanes < LOW, adapted[:half_low], prior[:half_low])
            bottom = jnp.where(lanes < LOW, adapted[half_low:], prior[self.grid - half_low :])
            spreads.append(jnp.concatenate([top, prior[inner], bottom], axis=0))
        return [
            [spreads[part] * noise_ref[move, 0, part] for part in range(PARTS)]
            for move in range(noise_ref.shape[0])
        ]

    def unrolled(self, drift, taken):
        gain, offset = 1.0, [jnp.zeros_like(value) for value in drift[0]]
        gains, offsets = [], []
        for step, accepted in zip(drift, taken):
            new_gain = self.keep * gain
            new_offset = [self.keep * old + value for old, value in zip(offset, step)]
            gains.append(new_gain)
            offsets.append(new_offset)
            gain = jnp.where(accepted, new_gain, gain)
            offset = [jnp.where(accepted, new, old) for new, old in zip(new_offset, offset)]
        return gains, offsets

    def folded(self, parts):
        half = self.half
        top = jnp.concatenate([part[:half] for part in parts], axis=1)
        high, rest = split(jnp.concatenate([part[half:] for part in parts], axis=1))
        other = dot(self.flip, high) + dot(self.flip, rest)
        even = top + jnp.where(self.first, 0.0, other)
        odd = jnp.where(self.first, other, self.turn(top - other))
        return jnp.concatenate([even, odd], axis=0)

    def fields(self, state):
        half, wave_x = self.half, self.wave_x
        psi = state * self.wide(0)
        even, odd = psi[:half], psi[half:]
        along_y = jnp.concatenate(
            [self.wave * odd, jnp.where(self.first, -float(half) * self.turn(odd), -self.wave * even)], axis=0
        )
        along_x = jnp.concatenate([wave_x * psi[:, half:], -wave_x * psi[:, :half]], axis=1)
        rows = [table_left(self.fold, value) for value in (state, along_y, along_x)]
        return table_right(jnp.concatenate(rows, axis=0), self.back)

    def scores(self, states, fields, observed_ref):
        grid, half, wave, wave_x = self.grid, self.half, self.wave, self.wave_x
        products = []
        for value in fields:
            vort = value[:grid]
            products += [value[grid : 2 * grid] * vort, value[2 * grid :] * vort]
        rows = table_right(jnp.concatenate(products, axis=0), self.fore)
        damping, flux_scale = self.wide(1), self.wide(2)
        finals = []
        for move, state in enumerate(states):
            flux_u = table_left(self.unfold, rows[(2 * move) * grid : (2 * move + 1) * grid])
            flux_v = table_left(self.unfold, rows[(2 * move + 1) * grid : (2 * move + 2) * grid])
            along_x = jnp.concatenate([-wave_x * flux_u[:, half:], wave_x * flux_u[:, :half]], axis=1)
            along_y = jnp.concatenate([wave * flux_v[half:], -wave * flux_v[:half]], axis=0)
            finals.append(table_left(self.fold, state * damping + flux_scale * (along_x + along_y)))
        forecast = table_right(jnp.concatenate(finals, axis=0), self.back)
        scale = 1.0 / (2.0 * noise_level * noise_level * grid * grid)
        result = []
        for move in range(len(states)):
            gap = forecast[move * grid : (move + 1) * grid] - observed_ref[...]
            result.append(jnp.sum(gap * gap) * scale)
        return result


def body(devices, particles, offspring, noise, accept, observed):
    groups = split_bits(devices)
    _, _, grid, half = particles.shape
    moves = noise.shape[0]
    assert particles.shape[0] == 1 and half == LANES and devices <= COUNT_ROWS * LANES
    copies = sum((1 << width) - 1 for _, width in groups)
    package = PARTS * LOW + COUNT_ROWS
    slots = TEAM + 2
    assert devices % TEAM == 0 and (PARTS * grid) % CHUNKS == 0
    chunk_shape = (CHUNKS, PARTS * grid // CHUNKS, half)
    tables = [jnp.asarray(table) for table in make_tables(grid)]
    hbm = pl.BlockSpec(memory_space=HBM)
    smem = pl.BlockSpec(memory_space=pltpu.SMEM)
    fetched = [noise, observed] + tables
    moved, misfit = pl.pallas_call(
        functools.partial(filter_kernel, devices, groups),
        out_shape=(
            jax.ShapeDtypeStruct((1, PARTS, grid, half), jnp.float32),
            jax.ShapeDtypeStruct((1, moves), jnp.float32),
        ),
        in_specs=[hbm, smem, smem] + [hbm] * len(fetched),
        out_specs=(pl.BlockSpec(memory_space=pltpu.VMEM), smem),
        scratch_shapes=[
            pltpu.VMEM((slots,) + chunk_shape, jnp.float32),
            pltpu.VMEM(chunk_shape, jnp.float32),
            pltpu.VMEM((len(groups) + 1, package, LANES), jnp.float32),
            pltpu.VMEM((copies, package, LANES), jnp.float32),
        ]
        + [pltpu.VMEM(value.shape, value.dtype) for value in fetched]
        + [
            pltpu.SemaphoreType.DMA,
            pltpu.SemaphoreType.DMA((2, 2)),
            pltpu.SemaphoreType.DMA((CHUNKS, 2)),
            pltpu.SemaphoreType.DMA((CHUNKS, 2)),
            pltpu.SemaphoreType.DMA((CHUNKS, 2)),
            pltpu.SemaphoreType.DMA((copies,)),
            pltpu.SemaphoreType.DMA((copies,)),
            pltpu.SemaphoreType.DMA((len(fetched),)),
        ],
        compiler_params=pltpu.CompilerParams(
            collective_id=0, has_side_effects=True, vmem_limit_bytes=63 * 1024 * 1024
        ),
        name="filter",
    )(particles.reshape(chunk_shape), offspring, accept.T, *fetched)
    return moved, misfit.T


def solution(mesh):
    return jax.shard_map(
        functools.partial(body, mesh.shape["dom"]),
        mesh=mesh,
        in_specs=(
            P("dom", None, None, None),
            P("dom"),
            P(None, "dom", None, None, None),
            P(None, "dom"),
            P(),
        ),
        out_specs=(P("dom", None, None, None), P(None, "dom")),
        check_vma=False,
    )
```

```python
import functools
import math

import jax
import jax.numpy as jnp
import ml_dtypes
import numpy as np
from jax import lax
from jax.experimental import pallas as pl
from jax.experimental.pallas import tpu as pltpu
from jax.sharding import PartitionSpec as P

REACH = 3
LOW = 16
LANES = 128
COUNT_LANE = 64
PARTS = 2
GROUP_BITS = 3
TEAM = 4
CHUNKS = 4

time_step = 0.05
viscosity = 0.001
noise_level = 0.5
spectral_scale = 64.0
prior_amplitude = 1.5
step_size = 0.4

MESH = pl.DeviceIdType.MESH
HBM = pltpu.MemorySpace.HBM


def split_bits(devices):
    bits = devices.bit_length() - 1
    assert 1 << bits == devices
    groups = []
    first = 0
    while first < bits:
        width = min(GROUP_BITS, bits - first)
        groups.append((first, width))
        first += width
    return groups


def filter_kernel(
    devices, groups, x_ref, count_ref, accept_ref, noise_hbm, observed_hbm, *rest
):
    tables_hbm = rest[:6]
    moved_ref, misfit_ref = rest[6:8]
    cand, chosen, sums, small, noise_ref, observed_ref = rest[8:14]
    tables = rest[14:20]
    load_sem, whole_sem, cross_sem, relay_sem, chosen_sem, small_send, small_recv, fetch_sem = rest[20:]
    chunks, chunk_rows, _ = x_ref.shape
    grid = chunks * chunk_rows // PARTS
    me = lax.axis_index("dom")
    place = lax.rem(me, TEAM)
    start = me - place
    core = lax.rem(place, 2)
    side = place // 2
    near = place + 1 - 2 * core
    across = lax.rem(place + 2, TEAM)
    both = lax.rem(near + 2, TEAM)
    sibling, partner = start + near, start + across
    chosen_to = me + TEAM - 2 * TEAM * side
    chosen_from = me - TEAM + 2 * TEAM * side
    sends_chosen = jnp.logical_and(chosen_to >= 0, chosen_to < devices)
    takes_chosen = jnp.logical_and(chosen_from >= 0, chosen_from < devices)
    far_to = jnp.where(place == 0, me - REACH, me + REACH)
    far_from = jnp.where(place == 1, me + REACH, me - REACH)
    outer = jnp.logical_or(place == 0, place == TEAM - 1)
    sends_far = jnp.logical_and(outer, jnp.logical_and(far_to >= 0, far_to < devices))
    takes_far = jnp.logical_and(
        jnp.logical_not(outer), jnp.logical_and(far_from >= 0, far_from < devices)
    )

    load = pltpu.make_async_copy(x_ref, cand.at[place], load_sem)
    load.start()
    fetches = [
        pltpu.make_async_copy(source, target, fetch_sem.at[at])
        for at, (source, target) in enumerate(
            zip((noise_hbm, observed_hbm) + tables_hbm, (noise_ref, observed_ref) + tables)
        )
    ]
    for fetch in fetches:
        fetch.start()

    barrier = pltpu.get_barrier_semaphore()

    def greet(device):
        pl.semaphore_signal(barrier, inc=1, device_id=(device,), device_id_type=MESH)

    partners = []
    for first, width in groups:
        partners.append([jnp.bitwise_xor(me, k << first) for k in range(1, 1 << width)])
    for group in partners:
        for device in group:
            greet(device)
    pl.when(takes_chosen)(lambda: greet(chosen_from))
    pl.when(takes_far)(lambda: greet(far_from))

    load.wait()
    count = count_ref[0].astype(jnp.float32)
    half_low = LOW // 2
    per_part = chunks // PARTS
    blocks = []
    for part in range(PARTS):
        blocks.append(cand[place, part * per_part, :half_low, :])
        blocks.append(cand[place, (part + 1) * per_part - 1, chunk_rows - half_low :, :])
    lane_ids = lax.broadcasted_iota(jnp.int32, (half_low, LANES), 1)
    row_ids = lax.broadcasted_iota(jnp.int32, (half_low, LANES), 0)
    counted = lane_ids >= COUNT_LANE
    order = jnp.where(counted, row_ids * (LANES - COUNT_LANE) + lane_ids - COUNT_LANE, devices)
    package = jnp.where(order == me, count, 0.0)
    for at, block in enumerate(blocks):
        value = block * block * count
        value = value if at == 0 else pltpu.roll(value, at * LOW, 1)
        inside = jnp.logical_and(lane_ids >= at * LOW, lane_ids < (at + 1) * LOW)
        package = jnp.where(inside, value, package)
    sums[0] = package

    expected = sum(len(group) for group in partners)
    pl.semaphore_wait(barrier, expected + sends_chosen.astype(jnp.int32) + sends_far.astype(jnp.int32))

    def remote(source, target, pair, device):
        return pltpu.make_async_remote_copy(
            src_ref=source,
            dst_ref=target,
            send_sem=pair.at[0],
            recv_sem=pair.at[1],
            device_id=(device,),
            device_id_type=MESH,
        )

    def stage_copies(stage):
        copies = []
        base = sum(len(group) for group in partners[:stage])
        for at, device in enumerate(partners[stage]):
            copies.append(
                pltpu.make_async_remote_copy(
                    src_ref=sums.at[stage],
                    dst_ref=small.at[base + at],
                    send_sem=small_send.at[base + at],
                    recv_sem=small_recv.at[base + at],
                    device_id=(device,),
                    device_id_type=MESH,
                )
            )
        return copies

    def cross(slot, chunk):
        return remote(cand.at[slot, chunk], cand.at[slot, chunk], cross_sem.at[chunk], partner)

    def relay(slot, chunk):
        return remote(cand.at[slot, chunk], cand.at[slot, chunk], relay_sem.at[chunk], sibling)

    def forward(chunk):
        return remote(chosen.at[chunk], cand.at[TEAM, chunk], chosen_sem.at[chunk], chosen_to)

    to_sibling = remote(cand.at[place], cand.at[place], whole_sem.at[0], sibling)
    from_sibling = remote(cand.at[near], cand.at[near], whole_sem.at[0], sibling)
    to_far = remote(cand.at[place], cand.at[TEAM + 1], whole_sem.at[1], far_to)

    first_stage = stage_copies(0)
    for copy in first_stage:
        copy.start()
    for chunk in range(chunks):
        cross(place, chunk).start()
    to_sibling.start()
    pl.when(sends_far)(to_far.start)

    def pass_on(chunk):
        cross(across, chunk).wait_recv()
        relay(across, chunk).start()

    stages = [first_stage]
    for stage in range(len(groups)):
        if stage > 0:
            stages.append(stage_copies(stage))
            for copy in stages[stage]:
                copy.start()
        if stage == len(groups) - 1:
            pass_on(0)
        base = sum(len(group) for group in partners[:stage])
        total = sums[stage]
        for at, copy in enumerate(stages[stage]):
            copy.wait_recv()
            total = total + small[base + at]
        sums[stage + 1] = total

    reduced = sums[len(groups)]
    counts = jnp.where(counted, reduced, 0.0)

    def source_place(slot):
        found = jnp.full((1, 1), 1.0, jnp.float32) * (slot - REACH - start).astype(jnp.float32)
        for distance in range(-REACH, REACH):
            ends = jnp.sum(jnp.where(order <= slot + distance, counts, 0.0), keepdims=True)
            found = found + jnp.where(ends <= slot.astype(jnp.float32), 1.0, 0.0)
        return jnp.broadcast_to(found, (chunk_rows, LANES))

    forward_place = source_place(chosen_to)
    from_sibling.wait_recv()

    def team_value(which, chunk):
        value = cand[0, chunk]
        for at in range(1, TEAM):
            value = jnp.where(which == at, cand[at, chunk], value)
        return value

    def send_chosen(chunk):
        relay(both, chunk).wait_recv()
        chosen[chunk] = team_value(forward_place, chunk)
        pl.when(sends_chosen)(forward(chunk).start)

    for chunk in range(1, chunks):
        pass_on(chunk)
        send_chosen(chunk - 1)
    send_chosen(chunks - 1)

    for fetch in fetches:
        fetch.wait()
    work = Work(devices, grid, tables)
    totals = [reduced if at == 0 else pltpu.roll(reduced, LANES - at * LOW, 1) for at in range(2 * PARTS)]
    drift = work.drifts(noise_ref, totals)
    taken = [accept_ref[0, move] == 1 for move in range(len(drift))]
    gains, offsets = work.unrolled(drift, taken)
    offset_states = [work.folded(value) for value in offsets]
    offset_fields = [work.fields(state) for state in offset_states]

    own_place = source_place(me)
    first_side = jnp.broadcast_to(jnp.full((1, 1), 1.0, jnp.float32) * side.astype(jnp.float32), (chunk_rows, LANES)) < 0.5
    before, after = own_place < 0.0, own_place > TEAM - 1.0
    use_chosen = jnp.logical_or(jnp.logical_and(first_side, before), jnp.logical_and(jnp.logical_not(first_side), after))
    use_far = jnp.logical_and(jnp.logical_or(before, after), jnp.logical_not(use_chosen))

    def arrived_far():
        remote(cand.at[TEAM + 1], cand.at[TEAM + 1], whole_sem.at[1], far_from).wait_recv()

    pl.when(takes_far)(arrived_far)
    pieces = []
    for chunk in range(chunks):
        def arrived():
            remote(chosen.at[chunk], cand.at[TEAM, chunk], chosen_sem.at[chunk], chosen_from).wait_recv()

        pl.when(takes_chosen)(arrived)
        value = team_value(own_place, chunk)
        value = jnp.where(use_chosen, cand[TEAM, chunk], value)
        pieces.append(jnp.where(use_far, cand[TEAM + 1, chunk], value))
    present = [jnp.concatenate(pieces[part * per_part : (part + 1) * per_part], axis=0) for part in range(PARTS)]

    moved = present
    for move in range(len(drift)):
        candidate = [work.keep * moved[part] + drift[move][part] for part in range(PARTS)]
        moved = [jnp.where(taken[move], candidate[part], moved[part]) for part in range(PARTS)]
    for part in range(PARTS):
        moved_ref[0, part] = moved[part]

    base_state = work.folded(present)
    base_fields = work.fields(base_state)
    states = [gain * base_state + state for gain, state in zip(gains, offset_states)]
    fields = [gain * base_fields + value for gain, value in zip(gains, offset_fields)]
    for move, score in enumerate(work.scores(states, fields, observed_ref)):
        misfit_ref[0, move] = score

    for copies in stages:
        for copy in copies:
            copy.wait_send()
    to_sibling.wait_send()
    pl.when(sends_far)(to_far.wait_send)
    for chunk in range(chunks):
        cross(place, chunk).wait_send()
        relay(across, chunk).wait_send()
        pl.when(sends_chosen)(forward(chunk).wait_send)


def halves(table):
    table = np.asarray(table, np.float64)
    high = table.astype(np.float32).astype(ml_dtypes.bfloat16)
    rest = (table - high.astype(np.float64)).astype(np.float32).astype(ml_dtypes.bfloat16)
    return np.stack([high, rest])


def make_tables(grid):
    half = grid // 2
    angle = 2.0 * math.pi / grid
    index = np.arange(grid)
    low = np.arange(half)
    phase = (index[:, None] * low[None, :] % grid) * angle
    sines = np.sin(phase)
    sines[:, 0] = 1.0 - 2.0 * (index % 2)
    fold = np.concatenate([np.cos(phase), sines], axis=1)
    weight = np.where(low == 0, 1.0, 2.0)[:, None]
    back = np.concatenate([weight * np.cos(phase).T, -weight * np.sin(phase).T], axis=0) / spectral_scale
    fore = np.concatenate([np.cos(phase), -np.sin(phase)], axis=1) * (spectral_scale / (grid * grid))
    flip = np.zeros((half, half))
    flip[low, (half - low) % half] = 1.0
    wave_y = np.concatenate([low, np.where(low == 0, half, low)]).astype(np.float64)[:, None]
    wave_x = low.astype(np.float64)[None, :]
    square = wave_y**2 + wave_x**2
    inverse = np.where(square > 0, 1.0 / np.maximum(square, 1.0), 0.0)
    damping = 1.0 / (1.0 + time_step * viscosity * square)
    keeper = (np.abs(wave_y) <= grid // 3) & (wave_x <= grid // 3)
    doubled = np.where(np.concatenate([low, low])[:, None] == 0, 1.0, 2.0)
    flux = -time_step * keeper * doubled * damping
    signed = np.where(index < half, index, index - grid).astype(np.float64)[:, None]
    prior = prior_amplitude / (1.0 + np.sqrt(signed**2 + wave_x**2) / 8.0)
    scales = np.stack([inverse, damping, flux, step_size * prior]).astype(np.float32)
    return (
        halves(fold), halves(fold.T), halves(back), halves(fore),
        flip.astype(ml_dtypes.bfloat16), scales,
    )


def split(value):
    high = value.astype(jnp.bfloat16)
    return high, (value - high.astype(jnp.float32)).astype(jnp.bfloat16)


def dot(a, b):
    return jnp.dot(a, b, preferred_element_type=jnp.float32)


def table_left(table, value):
    high, rest = split(value)
    return dot(table[0], high) + dot(table[0], rest) + dot(table[1], high)


def table_right(value, table):
    high, rest = split(value)
    return dot(high, table[0]) + dot(rest, table[0]) + dot(high, table[1])


class Work:
    def __init__(self, devices, grid, tables):
        fold, unfold, back, fore, flip, scales = tables
        self.devices, self.grid, self.half = devices, grid, grid // 2
        self.fold = (fold[0], fold[1])
        self.unfold = (unfold[0], unfold[1])
        self.back = (back[0], back[1])
        self.fore = (fore[0], fore[1])
        self.flip = flip[...]
        self.scales = scales
        self.keep = math.sqrt(1.0 - step_size * step_size)
        row_ids = lax.broadcasted_iota(jnp.int32, (self.half, grid), 0)
        self.first = row_ids == 0
        self.wave = row_ids.astype(jnp.float32)
        self.wave_x = lax.broadcasted_iota(jnp.int32, (grid, self.half), 1).astype(jnp.float32)

    def wide(self, index):
        value = self.scales[index]
        return jnp.concatenate([value, value], axis=1)

    def turn(self, value):
        return jnp.concatenate([-value[:, self.half :], value[:, : self.half]], axis=1)

    def drifts(self, noise_ref, totals):
        half_low = LOW // 2
        lanes = lax.broadcasted_iota(jnp.int32, (half_low, self.half), 1)
        prior = self.scales[3]
        inner = slice(half_low, self.grid - half_low)
        spreads = []
        for part in range(PARTS):
            head, tail = [
                step_size * jnp.sqrt(total * (1.0 / self.devices) + 1e-06)
                for total in totals[2 * part : 2 * part + 2]
            ]
            top = jnp.where(lanes < LOW, head, prior[:half_low])
            bottom = jnp.where(lanes < LOW, tail, prior[self.grid - half_low :])
            spreads.append(jnp.concatenate([top, prior[inner], bottom], axis=0))
        return [
            [spreads[part] * noise_ref[move, 0, part] for part in range(PARTS)]
            for move in range(noise_ref.shape[0])
        ]

    def unrolled(self, drift, taken):
        gain, offset = 1.0, [jnp.zeros_like(value) for value in drift[0]]
        gains, offsets = [], []
        for step, accepted in zip(drift, taken):
            new_gain = self.keep * gain
            new_offset = [self.keep * old + value for old, value in zip(offset, step)]
            gains.append(new_gain)
            offsets.append(new_offset)
            gain = jnp.where(accepted, new_gain, gain)
            offset = [jnp.where(accepted, new, old) for new, old in zip(new_offset, offset)]
        return gains, offsets

    def folded(self, parts):
        half = self.half
        top = jnp.concatenate([part[:half] for part in parts], axis=1)
        high, rest = split(jnp.concatenate([part[half:] for part in parts], axis=1))
        other = dot(self.flip, high) + dot(self.flip, rest)
        even = top + jnp.where(self.first, 0.0, other)
        odd = jnp.where(self.first, other, self.turn(top - other))
        return jnp.concatenate([even, odd], axis=0)

    def fields(self, state):
        half, wave_x = self.half, self.wave_x
        psi = state * self.wide(0)
        even, odd = psi[:half], psi[half:]
        along_y = jnp.concatenate(
            [self.wave * odd, jnp.where(self.first, -float(half) * self.turn(odd), -self.wave * even)], axis=0
        )
        along_x = jnp.concatenate([wave_x * psi[:, half:], -wave_x * psi[:, :half]], axis=1)
        rows = [table_left(self.fold, value) for value in (state, along_y, along_x)]
        return table_right(jnp.concatenate(rows, axis=0), self.back)

    def scores(self, states, fields, observed_ref):
        grid, half, wave, wave_x = self.grid, self.half, self.wave, self.wave_x
        products = []
        for value in fields:
            vort = value[:grid]
            products += [value[grid : 2 * grid] * vort, value[2 * grid :] * vort]
        rows = table_right(jnp.concatenate(products, axis=0), self.fore)
        damping, flux_scale = self.wide(1), self.wide(2)
        finals = []
        for move, state in enumerate(states):
            flux_u = table_left(self.unfold, rows[(2 * move) * grid : (2 * move + 1) * grid])
            flux_v = table_left(self.unfold, rows[(2 * move + 1) * grid : (2 * move + 2) * grid])
            along_x = jnp.concatenate([-wave_x * flux_u[:, half:], wave_x * flux_u[:, :half]], axis=1)
            along_y = jnp.concatenate([wave * flux_v[half:], -wave * flux_v[:half]], axis=0)
            finals.append(table_left(self.fold, state * damping + flux_scale * (along_x + along_y)))
        forecast = table_right(jnp.concatenate(finals, axis=0), self.back)
        scale = 1.0 / (2.0 * noise_level * noise_level * grid * grid)
        result = []
        for move in range(len(states)):
            gap = forecast[move * grid : (move + 1) * grid] - observed_ref[...]
            result.append(jnp.sum(gap * gap) * scale)
        return result


def settle_kernel(moved_ref, misfit_ref, moved_out, misfit_out, sems):
    pieces = sems.shape[0]
    parts, rows = moved_ref.shape[1], moved_ref.shape[2]
    span = parts * rows // pieces
    per_part = pieces // parts
    copies = []
    for at in range(pieces):
        where = (0, at // per_part, pl.ds(at % per_part * span, span))
        copies.append(pltpu.make_async_copy(moved_ref.at[where], moved_out.at[where], sems.at[at]))
    for copy in copies:
        copy.start()
    for move in range(misfit_ref.shape[1]):
        misfit_out[0, move] = misfit_ref[0, move]
    for copy in copies:
        copy.wait()


def settle(moved, misfit):
    hbm = pl.BlockSpec(memory_space=HBM)
    smem = pl.BlockSpec(memory_space=pltpu.SMEM)
    return pl.pallas_call(
        settle_kernel,
        out_shape=tuple(jax.ShapeDtypeStruct(value.shape, value.dtype) for value in (moved, misfit)),
        in_specs=[hbm, smem],
        out_specs=(hbm, smem),
        scratch_shapes=[pltpu.SemaphoreType.DMA((CHUNKS,))],
        compiler_params=pltpu.CompilerParams(vmem_limit_bytes=63 * 1024 * 1024),
        name="settle",
    )(moved, misfit)


def body(devices, particles, offspring, noise, accept, observed):
    groups = split_bits(devices)
    _, _, grid, half = particles.shape
    moves = noise.shape[0]
    assert particles.shape[0] == 1 and half == LANES and devices <= LOW // 2 * (LANES - COUNT_LANE)
    copies = sum((1 << width) - 1 for _, width in groups)
    package = LOW // 2
    assert 2 * PARTS * LOW == COUNT_LANE
    slots = TEAM + 2
    assert devices % TEAM == 0 and (PARTS * grid) % CHUNKS == 0
    chunk_shape = (CHUNKS, PARTS * grid // CHUNKS, half)
    tables = [jnp.asarray(table) for table in make_tables(grid)]
    hbm = pl.BlockSpec(memory_space=HBM)
    smem = pl.BlockSpec(memory_space=pltpu.SMEM)
    fetched = [noise, observed] + tables
    moved, misfit = pl.pallas_call(
        functools.partial(filter_kernel, devices, groups),
        out_shape=(
            jax.ShapeDtypeStruct((1, PARTS, grid, half), jnp.float32),
            jax.ShapeDtypeStruct((1, moves), jnp.float32),
        ),
        in_specs=[hbm, smem, smem] + [hbm] * len(fetched),
        out_specs=(pl.BlockSpec(memory_space=pltpu.VMEM), smem),
        scratch_shapes=[
            pltpu.VMEM((slots,) + chunk_shape, jnp.float32),
            pltpu.VMEM(chunk_shape, jnp.float32),
            pltpu.VMEM((len(groups) + 1, package, LANES), jnp.float32),
            pltpu.VMEM((copies, package, LANES), jnp.float32),
        ]
        + [pltpu.VMEM(value.shape, value.dtype) for value in fetched]
        + [
            pltpu.SemaphoreType.DMA,
            pltpu.SemaphoreType.DMA((2, 2)),
            pltpu.SemaphoreType.DMA((CHUNKS, 2)),
            pltpu.SemaphoreType.DMA((CHUNKS, 2)),
            pltpu.SemaphoreType.DMA((CHUNKS, 2)),
            pltpu.SemaphoreType.DMA((copies,)),
            pltpu.SemaphoreType.DMA((copies,)),
            pltpu.SemaphoreType.DMA((len(fetched),)),
        ],
        compiler_params=pltpu.CompilerParams(
            collective_id=0, has_side_effects=True, vmem_limit_bytes=63 * 1024 * 1024
        ),
        name="filter",
    )(particles.reshape(chunk_shape), offspring, accept.T, *fetched)
    moved, misfit = settle(moved, misfit)
    return moved, misfit.T


def solution(mesh):
    return jax.shard_map(
        functools.partial(body, mesh.shape["dom"]),
        mesh=mesh,
        in_specs=(
            P("dom", None, None, None),
            P("dom"),
            P(None, "dom", None, None, None),
            P(None, "dom"),
            P(),
        ),
        out_specs=(P("dom", None, None, None), P(None, "dom")),
        check_vma=False,
    )
```

```python
import functools
import math

import jax
import jax.numpy as jnp
import ml_dtypes
import numpy as np
from jax import lax
from jax.experimental import pallas as pl
from jax.experimental.pallas import tpu as pltpu
from jax.sharding import PartitionSpec as P

REACH = 3
LOW = 16
LANES = 128
COUNT_LANE = 64
PARTS = 2
GROUP_BITS = 3
TEAM = 4
CHUNKS = 8
PIECES = 4

time_step = 0.05
viscosity = 0.001
noise_level = 0.5
spectral_scale = 64.0
prior_amplitude = 1.5
step_size = 0.4

MESH = pl.DeviceIdType.MESH
HBM = pltpu.MemorySpace.HBM


def split_bits(devices):
    bits = devices.bit_length() - 1
    assert 1 << bits == devices
    groups = []
    first = 0
    while first < bits:
        width = min(GROUP_BITS, bits - first)
        groups.append((first, width))
        first += width
    return groups


def filter_kernel(
    devices, groups, x_ref, count_ref, accept_ref, noise_hbm, observed_hbm, *rest
):
    tables_hbm = rest[:6]
    moved_ref, misfit_ref = rest[6:8]
    cand, chosen, sums, small, moved_stage, noise_ref, observed_ref = rest[8:15]
    tables = rest[15:21]
    load_sem, whole_sem, cross_sem, relay_sem, chosen_sem, small_send, small_recv, fetch_sem = rest[21:]
    chunks, chunk_rows, _ = x_ref.shape
    grid = chunks * chunk_rows // PARTS
    me = lax.axis_index("dom")
    place = lax.rem(me, TEAM)
    start = me - place
    core = lax.rem(place, 2)
    side = place // 2
    near = place + 1 - 2 * core
    across = lax.rem(place + 2, TEAM)
    both = lax.rem(near + 2, TEAM)
    sibling, partner = start + near, start + across
    chosen_to = me + TEAM - 2 * TEAM * side
    chosen_from = me - TEAM + 2 * TEAM * side
    sends_chosen = jnp.logical_and(chosen_to >= 0, chosen_to < devices)
    takes_chosen = jnp.logical_and(chosen_from >= 0, chosen_from < devices)
    far_to = jnp.where(place == 0, me - REACH, me + REACH)
    far_from = jnp.where(place == 1, me + REACH, me - REACH)
    outer = jnp.logical_or(place == 0, place == TEAM - 1)
    sends_far = jnp.logical_and(outer, jnp.logical_and(far_to >= 0, far_to < devices))
    takes_far = jnp.logical_and(
        jnp.logical_not(outer), jnp.logical_and(far_from >= 0, far_from < devices)
    )

    load = pltpu.make_async_copy(x_ref, cand.at[place], load_sem)
    load.start()
    fetches = [
        pltpu.make_async_copy(source, target, fetch_sem.at[at])
        for at, (source, target) in enumerate(
            zip((noise_hbm, observed_hbm) + tables_hbm, (noise_ref, observed_ref) + tables)
        )
    ]
    for fetch in fetches:
        fetch.start()

    barrier = pltpu.get_barrier_semaphore()

    def greet(device):
        pl.semaphore_signal(barrier, inc=1, device_id=(device,), device_id_type=MESH)

    partners = []
    for first, width in groups:
        partners.append([jnp.bitwise_xor(me, k << first) for k in range(1, 1 << width)])
    for group in partners:
        for device in group:
            greet(device)
    pl.when(takes_chosen)(lambda: greet(chosen_from))
    pl.when(takes_far)(lambda: greet(far_from))

    load.wait()
    count = count_ref[0].astype(jnp.float32)
    half_low = LOW // 2
    per_part = chunks // PARTS
    blocks = []
    for part in range(PARTS):
        blocks.append(cand[place, part * per_part, :half_low, :])
        blocks.append(cand[place, (part + 1) * per_part - 1, chunk_rows - half_low :, :])
    lane_ids = lax.broadcasted_iota(jnp.int32, (half_low, LANES), 1)
    row_ids = lax.broadcasted_iota(jnp.int32, (half_low, LANES), 0)
    counted = lane_ids >= COUNT_LANE
    order = jnp.where(counted, row_ids * (LANES - COUNT_LANE) + lane_ids - COUNT_LANE, devices)
    package = jnp.where(order == me, count, 0.0)
    for at, block in enumerate(blocks):
        value = block * block * count
        value = value if at == 0 else pltpu.roll(value, at * LOW, 1)
        inside = jnp.logical_and(lane_ids >= at * LOW, lane_ids < (at + 1) * LOW)
        package = jnp.where(inside, value, package)
    sums[0] = package

    expected = sum(len(group) for group in partners)
    pl.semaphore_wait(barrier, expected + sends_chosen.astype(jnp.int32) + sends_far.astype(jnp.int32))

    def remote(source, target, pair, device):
        return pltpu.make_async_remote_copy(
            src_ref=source,
            dst_ref=target,
            send_sem=pair.at[0],
            recv_sem=pair.at[1],
            device_id=(device,),
            device_id_type=MESH,
        )

    def stage_copies(stage):
        copies = []
        base = sum(len(group) for group in partners[:stage])
        for at, device in enumerate(partners[stage]):
            copies.append(
                pltpu.make_async_remote_copy(
                    src_ref=sums.at[stage],
                    dst_ref=small.at[base + at],
                    send_sem=small_send.at[base + at],
                    recv_sem=small_recv.at[base + at],
                    device_id=(device,),
                    device_id_type=MESH,
                )
            )
        return copies

    def cross(slot, chunk):
        return remote(cand.at[slot, chunk], cand.at[slot, chunk], cross_sem.at[chunk], partner)

    def relay(slot, chunk):
        return remote(cand.at[slot, chunk], cand.at[slot, chunk], relay_sem.at[chunk], sibling)

    def forward(chunk):
        return remote(chosen.at[chunk], cand.at[TEAM, chunk], chosen_sem.at[chunk], chosen_to)

    to_sibling = remote(cand.at[place], cand.at[place], whole_sem.at[0], sibling)
    from_sibling = remote(cand.at[near], cand.at[near], whole_sem.at[0], sibling)
    to_far = remote(cand.at[place], cand.at[TEAM + 1], whole_sem.at[1], far_to)

    first_stage = stage_copies(0)
    for copy in first_stage:
        copy.start()
    for chunk in range(chunks):
        cross(place, chunk).start()
    to_sibling.start()
    pl.when(sends_far)(to_far.start)

    def pass_on(chunk):
        cross(across, chunk).wait_recv()
        relay(across, chunk).start()

    stages = [first_stage]
    for stage in range(len(groups)):
        if stage > 0:
            stages.append(stage_copies(stage))
            for copy in stages[stage]:
                copy.start()
        if stage == len(groups) - 1:
            pass_on(0)
        base = sum(len(group) for group in partners[:stage])
        total = sums[stage]
        for at, copy in enumerate(stages[stage]):
            copy.wait_recv()
            total = total + small[base + at]
        sums[stage + 1] = total

    reduced = sums[len(groups)]
    counts = jnp.where(counted, reduced, 0.0)

    def source_place(slot):
        found = jnp.full((1, 1), 1.0, jnp.float32) * (slot - REACH - start).astype(jnp.float32)
        for distance in range(-REACH, REACH):
            ends = jnp.sum(jnp.where(order <= slot + distance, counts, 0.0), keepdims=True)
            found = found + jnp.where(ends <= slot.astype(jnp.float32), 1.0, 0.0)
        return jnp.broadcast_to(found, (chunk_rows, LANES))

    forward_place = source_place(chosen_to)
    from_sibling.wait_recv()

    def team_value(which, chunk):
        value = cand[0, chunk]
        for at in range(1, TEAM):
            value = jnp.where(which == at, cand[at, chunk], value)
        return value

    def send_chosen(chunk):
        relay(both, chunk).wait_recv()
        chosen[chunk] = team_value(forward_place, chunk)
        pl.when(sends_chosen)(forward(chunk).start)

    for chunk in range(1, chunks):
        pass_on(chunk)
        send_chosen(chunk - 1)
    send_chosen(chunks - 1)

    for fetch in fetches:
        fetch.wait()
    work = Work(devices, grid, tables)
    totals = [reduced if at == 0 else pltpu.roll(reduced, LANES - at * LOW, 1) for at in range(2 * PARTS)]
    drift = work.drifts(noise_ref, totals)
    taken = [accept_ref[0, move] == 1 for move in range(len(drift))]
    gains, offsets = work.unrolled(drift, taken)
    offset_states = [work.folded(value) for value in offsets]
    offset_fields = [work.fields(state) for state in offset_states]

    own_place = source_place(me)
    first_side = jnp.broadcast_to(jnp.full((1, 1), 1.0, jnp.float32) * side.astype(jnp.float32), (chunk_rows, LANES)) < 0.5
    before, after = own_place < 0.0, own_place > TEAM - 1.0
    use_chosen = jnp.logical_or(jnp.logical_and(first_side, before), jnp.logical_and(jnp.logical_not(first_side), after))
    use_far = jnp.logical_and(jnp.logical_or(before, after), jnp.logical_not(use_chosen))

    def arrived_far():
        remote(cand.at[TEAM + 1], cand.at[TEAM + 1], whole_sem.at[1], far_from).wait_recv()

    pl.when(takes_far)(arrived_far)
    pieces = []
    for chunk in range(chunks):
        def arrived():
            remote(chosen.at[chunk], cand.at[TEAM, chunk], chosen_sem.at[chunk], chosen_from).wait_recv()

        pl.when(takes_chosen)(arrived)
        value = team_value(own_place, chunk)
        value = jnp.where(use_chosen, cand[TEAM, chunk], value)
        pieces.append(jnp.where(use_far, cand[TEAM + 1, chunk], value))
    present = [jnp.concatenate(pieces[part * per_part : (part + 1) * per_part], axis=0) for part in range(PARTS)]

    moved = present
    for move in range(len(drift)):
        candidate = [work.keep * moved[part] + drift[move][part] for part in range(PARTS)]
        moved = [jnp.where(taken[move], candidate[part], moved[part]) for part in range(PARTS)]
    for part in range(PARTS):
        moved_stage[0, part] = moved[part]
    leave = pltpu.make_async_copy(moved_stage, moved_ref, load_sem)
    leave.start()

    base_state = work.folded(present)
    base_fields = work.fields(base_state)
    states = [gain * base_state + state for gain, state in zip(gains, offset_states)]
    fields = [gain * base_fields + value for gain, value in zip(gains, offset_fields)]
    for move, score in enumerate(work.scores(states, fields, observed_ref)):
        misfit_ref[0, move] = score

    leave.wait()
    for copies in stages:
        for copy in copies:
            copy.wait_send()
    to_sibling.wait_send()
    pl.when(sends_far)(to_far.wait_send)
    for chunk in range(chunks):
        cross(place, chunk).wait_send()
        relay(across, chunk).wait_send()
        pl.when(sends_chosen)(forward(chunk).wait_send)


def halves(table):
    table = np.asarray(table, np.float64)
    high = table.astype(np.float32).astype(ml_dtypes.bfloat16)
    rest = (table - high.astype(np.float64)).astype(np.float32).astype(ml_dtypes.bfloat16)
    return np.stack([high, rest])


def make_tables(grid):
    half = grid // 2
    angle = 2.0 * math.pi / grid
    index = np.arange(grid)
    low = np.arange(half)
    phase = (index[:, None] * low[None, :] % grid) * angle
    sines = np.sin(phase)
    sines[:, 0] = 1.0 - 2.0 * (index % 2)
    fold = np.concatenate([np.cos(phase), sines], axis=1)
    weight = np.where(low == 0, 1.0, 2.0)[:, None]
    back = np.concatenate([weight * np.cos(phase).T, -weight * np.sin(phase).T], axis=0) / spectral_scale
    fore = np.concatenate([np.cos(phase), -np.sin(phase)], axis=1) * (spectral_scale / (grid * grid))
    flip = np.zeros((half, half))
    flip[low, (half - low) % half] = 1.0
    wave_y = np.concatenate([low, np.where(low == 0, half, low)]).astype(np.float64)[:, None]
    wave_x = low.astype(np.float64)[None, :]
    square = wave_y**2 + wave_x**2
    inverse = np.where(square > 0, 1.0 / np.maximum(square, 1.0), 0.0)
    damping = 1.0 / (1.0 + time_step * viscosity * square)
    keeper = (np.abs(wave_y) <= grid // 3) & (wave_x <= grid // 3)
    doubled = np.where(np.concatenate([low, low])[:, None] == 0, 1.0, 2.0)
    flux = -time_step * keeper * doubled * damping
    signed = np.where(index < half, index, index - grid).astype(np.float64)[:, None]
    prior = prior_amplitude / (1.0 + np.sqrt(signed**2 + wave_x**2) / 8.0)
    scales = np.stack([inverse, damping, flux, step_size * prior]).astype(np.float32)
    return (
        halves(fold), halves(fold.T), halves(back), halves(fore),
        flip.astype(ml_dtypes.bfloat16), scales,
    )


def split(value):
    high = value.astype(jnp.bfloat16)
    return high, (value - high.astype(jnp.float32)).astype(jnp.bfloat16)


def dot(a, b):
    return jnp.dot(a, b, preferred_element_type=jnp.float32)


def table_left(table, value):
    high, rest = split(value)
    return dot(table[0], high) + dot(table[0], rest) + dot(table[1], high)


def table_right(value, table):
    high, rest = split(value)
    return dot(high, table[0]) + dot(rest, table[0]) + dot(high, table[1])


class Work:
    def __init__(self, devices, grid, tables):
        fold, unfold, back, fore, flip, scales = tables
        self.devices, self.grid, self.half = devices, grid, grid // 2
        self.fold = (fold[0], fold[1])
        self.unfold = (unfold[0], unfold[1])
        self.back = (back[0], back[1])
        self.fore = (fore[0], fore[1])
        self.flip = flip[...]
        self.scales = scales
        self.keep = math.sqrt(1.0 - step_size * step_size)
        row_ids = lax.broadcasted_iota(jnp.int32, (self.half, grid), 0)
        self.first = row_ids == 0
        self.wave = row_ids.astype(jnp.float32)
        self.wave_x = lax.broadcasted_iota(jnp.int32, (grid, self.half), 1).astype(jnp.float32)

    def wide(self, index):
        value = self.scales[index]
        return jnp.concatenate([value, value], axis=1)

    def turn(self, value):
        return jnp.concatenate([-value[:, self.half :], value[:, : self.half]], axis=1)

    def drifts(self, noise_ref, totals):
        half_low = LOW // 2
        lanes = lax.broadcasted_iota(jnp.int32, (half_low, self.half), 1)
        prior = self.scales[3]
        inner = slice(half_low, self.grid - half_low)
        spreads = []
        for part in range(PARTS):
            head, tail = [
                step_size * jnp.sqrt(total * (1.0 / self.devices) + 1e-06)
                for total in totals[2 * part : 2 * part + 2]
            ]
            top = jnp.where(lanes < LOW, head, prior[:half_low])
            bottom = jnp.where(lanes < LOW, tail, prior[self.grid - half_low :])
            spreads.append(jnp.concatenate([top, prior[inner], bottom], axis=0))
        return [
            [spreads[part] * noise_ref[move, 0, part] for part in range(PARTS)]
            for move in range(noise_ref.shape[0])
        ]

    def unrolled(self, drift, taken):
        gain, offset = 1.0, [jnp.zeros_like(value) for value in drift[0]]
        gains, offsets = [], []
        for step, accepted in zip(drift, taken):
            new_gain = self.keep * gain
            new_offset = [self.keep * old + value for old, value in zip(offset, step)]
            gains.append(new_gain)
            offsets.append(new_offset)
            gain = jnp.where(accepted, new_gain, gain)
            offset = [jnp.where(accepted, new, old) for new, old in zip(new_offset, offset)]
        return gains, offsets

    def folded(self, parts):
        half = self.half
        top = jnp.concatenate([part[:half] for part in parts], axis=1)
        high, rest = split(jnp.concatenate([part[half:] for part in parts], axis=1))
        other = dot(self.flip, high) + dot(self.flip, rest)
        even = top + jnp.where(self.first, 0.0, other)
        odd = jnp.where(self.first, other, self.turn(top - other))
        return jnp.concatenate([even, odd], axis=0)

    def fields(self, state):
        half, wave_x = self.half, self.wave_x
        psi = state * self.wide(0)
        even, odd = psi[:half], psi[half:]
        along_y = jnp.concatenate(
            [self.wave * odd, jnp.where(self.first, -float(half) * self.turn(odd), -self.wave * even)], axis=0
        )
        along_x = jnp.concatenate([wave_x * psi[:, half:], -wave_x * psi[:, :half]], axis=1)
        rows = [table_left(self.fold, value) for value in (state, along_y, along_x)]
        return table_right(jnp.concatenate(rows, axis=0), self.back)

    def scores(self, states, fields, observed_ref):
        grid, half, wave, wave_x = self.grid, self.half, self.wave, self.wave_x
        products = []
        for value in fields:
            vort = value[:grid]
            products += [value[grid : 2 * grid] * vort, value[2 * grid :] * vort]
        rows = table_right(jnp.concatenate(products, axis=0), self.fore)
        damping, flux_scale = self.wide(1), self.wide(2)
        finals = []
        for move, state in enumerate(states):
            flux_u = table_left(self.unfold, rows[(2 * move) * grid : (2 * move + 1) * grid])
            flux_v = table_left(self.unfold, rows[(2 * move + 1) * grid : (2 * move + 2) * grid])
            along_x = jnp.concatenate([-wave_x * flux_u[:, half:], wave_x * flux_u[:, :half]], axis=1)
            along_y = jnp.concatenate([wave * flux_v[half:], -wave * flux_v[:half]], axis=0)
            finals.append(table_left(self.fold, state * damping + flux_scale * (along_x + along_y)))
        forecast = table_right(jnp.concatenate(finals, axis=0), self.back)
        scale = 1.0 / (2.0 * noise_level * noise_level * grid * grid)
        result = []
        for move in range(len(states)):
            gap = forecast[move * grid : (move + 1) * grid] - observed_ref[...]
            result.append(jnp.sum(gap * gap) * scale)
        return result


def settle_kernel(moved_ref, misfit_ref, moved_out, misfit_out, stage, sems):
    pieces = sems.shape[1]
    parts, rows = moved_ref.shape[1], moved_ref.shape[2]
    span = parts * rows // pieces
    per_part = pieces // parts
    reads, writes = [], []
    for at in range(pieces):
        where = (0, at // per_part, pl.ds(at % per_part * span, span))
        reads.append(pltpu.make_async_copy(moved_ref.at[where], stage.at[at], sems.at[0, at]))
        writes.append(pltpu.make_async_copy(stage.at[at], moved_out.at[where], sems.at[1, at]))
    for copy in reads:
        copy.start()
    for move in range(misfit_ref.shape[1]):
        misfit_out[0, move] = misfit_ref[0, move]
    for read, write in zip(reads, writes):
        read.wait()
        write.start()
    for copy in writes:
        copy.wait()


def settle(moved, misfit):
    hbm = pl.BlockSpec(memory_space=HBM)
    smem = pl.BlockSpec(memory_space=pltpu.SMEM)
    return pl.pallas_call(
        settle_kernel,
        out_shape=tuple(jax.ShapeDtypeStruct(value.shape, value.dtype) for value in (moved, misfit)),
        in_specs=[hbm, smem],
        out_specs=(hbm, smem),
        scratch_shapes=[
            pltpu.VMEM((PIECES, moved.shape[1] * moved.shape[2] // PIECES, moved.shape[3]), moved.dtype),
            pltpu.SemaphoreType.DMA((2, PIECES)),
        ],
        compiler_params=pltpu.CompilerParams(vmem_limit_bytes=63 * 1024 * 1024),
        name="settle",
    )(moved, misfit)


def body(devices, particles, offspring, noise, accept, observed):
    groups = split_bits(devices)
    _, _, grid, half = particles.shape
    moves = noise.shape[0]
    assert particles.shape[0] == 1 and half == LANES and devices <= LOW // 2 * (LANES - COUNT_LANE)
    copies = sum((1 << width) - 1 for _, width in groups)
    package = LOW // 2
    assert 2 * PARTS * LOW == COUNT_LANE
    slots = TEAM + 2
    assert devices % TEAM == 0 and (PARTS * grid) % CHUNKS == 0
    chunk_shape = (CHUNKS, PARTS * grid // CHUNKS, half)
    tables = [jnp.asarray(table) for table in make_tables(grid)]
    hbm = pl.BlockSpec(memory_space=HBM)
    smem = pl.BlockSpec(memory_space=pltpu.SMEM)
    fetched = [noise, observed] + tables
    moved, misfit = pl.pallas_call(
        functools.partial(filter_kernel, devices, groups),
        out_shape=(
            jax.ShapeDtypeStruct((1, PARTS, grid, half), jnp.float32),
            jax.ShapeDtypeStruct((1, moves), jnp.float32),
        ),
        in_specs=[hbm, smem, smem] + [hbm] * len(fetched),
        out_specs=(hbm, smem),
        scratch_shapes=[
            pltpu.VMEM((slots,) + chunk_shape, jnp.float32),
            pltpu.VMEM(chunk_shape, jnp.float32),
            pltpu.VMEM((len(groups) + 1, package, LANES), jnp.float32),
            pltpu.VMEM((copies, package, LANES), jnp.float32),
            pltpu.VMEM((1, PARTS, grid, half), jnp.float32),
        ]
        + [pltpu.VMEM(value.shape, value.dtype) for value in fetched]
        + [
            pltpu.SemaphoreType.DMA,
            pltpu.SemaphoreType.DMA((2, 2)),
            pltpu.SemaphoreType.DMA((CHUNKS, 2)),
            pltpu.SemaphoreType.DMA((CHUNKS, 2)),
            pltpu.SemaphoreType.DMA((CHUNKS, 2)),
            pltpu.SemaphoreType.DMA((copies,)),
            pltpu.SemaphoreType.DMA((copies,)),
            pltpu.SemaphoreType.DMA((len(fetched),)),
        ],
        compiler_params=pltpu.CompilerParams(
            collective_id=0, has_side_effects=True, vmem_limit_bytes=63 * 1024 * 1024
        ),
        name="filter",
    )(particles.reshape(chunk_shape), offspring, accept.T, *fetched)
    moved, misfit = settle(moved, misfit)
    return moved, misfit.T


def solution(mesh):
    return jax.shard_map(
        functools.partial(body, mesh.shape["dom"]),
        mesh=mesh,
        in_specs=(
            P("dom", None, None, None),
            P("dom"),
            P(None, "dom", None, None, None),
            P(None, "dom"),
            P(),
        ),
        out_specs=(P("dom", None, None, None), P(None, "dom")),
        check_vma=False,
    )
```

```python
import functools
import math

import jax
import jax.numpy as jnp
import ml_dtypes
import numpy as np
from jax import lax
from jax.experimental import pallas as pl
from jax.experimental.pallas import tpu as pltpu
from jax.sharding import PartitionSpec as P

REACH = 3
LOW = 16
LANES = 128
COUNT_LANE = 64
PARTS = 2
GROUP_BITS = 3
TEAM = 4
CHUNKS = 4

time_step = 0.05
viscosity = 0.001
noise_level = 0.5
spectral_scale = 64.0
prior_amplitude = 1.5
step_size = 0.4

MESH = pl.DeviceIdType.MESH
HBM = pltpu.MemorySpace.HBM


def split_bits(devices):
    bits = devices.bit_length() - 1
    assert 1 << bits == devices
    groups = []
    first = 0
    while first < bits:
        width = min(GROUP_BITS, bits - first)
        groups.append((first, width))
        first += width
    return groups


def filter_kernel(
    devices, groups, x_ref, count_ref, accept_ref, noise_hbm, observed_hbm, *rest
):
    tables_hbm = rest[:6]
    moved_ref, misfit_ref = rest[6:8]
    cand, chosen, sums, small, moved_stage, noise_ref, observed_ref = rest[8:15]
    tables = rest[15:21]
    load_sem, whole_sem, cross_sem, relay_sem, chosen_sem, small_send, small_recv, fetch_sem = rest[21:]
    chunks, chunk_rows, _ = x_ref.shape
    grid = chunks * chunk_rows // PARTS
    me = lax.axis_index("dom")
    place = lax.rem(me, TEAM)
    start = me - place
    core = lax.rem(place, 2)
    side = place // 2
    near = place + 1 - 2 * core
    across = lax.rem(place + 2, TEAM)
    both = lax.rem(near + 2, TEAM)
    sibling, partner = start + near, start + across
    chosen_to = me + TEAM - 2 * TEAM * side
    chosen_from = me - TEAM + 2 * TEAM * side
    sends_chosen = jnp.logical_and(chosen_to >= 0, chosen_to < devices)
    takes_chosen = jnp.logical_and(chosen_from >= 0, chosen_from < devices)
    far_to = jnp.where(place == 0, me - REACH, me + REACH)
    far_from = jnp.where(place == 1, me + REACH, me - REACH)
    outer = jnp.logical_or(place == 0, place == TEAM - 1)
    sends_far = jnp.logical_and(outer, jnp.logical_and(far_to >= 0, far_to < devices))
    takes_far = jnp.logical_and(
        jnp.logical_not(outer), jnp.logical_and(far_from >= 0, far_from < devices)
    )

    load = pltpu.make_async_copy(x_ref, cand.at[place], load_sem)
    load.start()
    fetches = [
        pltpu.make_async_copy(source, target, fetch_sem.at[at])
        for at, (source, target) in enumerate(
            zip((noise_hbm, observed_hbm) + tables_hbm, (noise_ref, observed_ref) + tables)
        )
    ]
    barrier = pltpu.get_barrier_semaphore()

    def greet(device):
        pl.semaphore_signal(barrier, inc=1, device_id=(device,), device_id_type=MESH)

    partners = []
    for first, width in groups:
        partners.append([jnp.bitwise_xor(me, k << first) for k in range(1, 1 << width)])
    for group in partners:
        for device in group:
            greet(device)
    pl.when(takes_chosen)(lambda: greet(chosen_from))
    pl.when(takes_far)(lambda: greet(far_from))

    load.wait()
    count = count_ref[0].astype(jnp.float32)
    half_low = LOW // 2
    per_part = chunks // PARTS
    blocks = []
    for part in range(PARTS):
        blocks.append(cand[place, part * per_part, :half_low, :])
        blocks.append(cand[place, (part + 1) * per_part - 1, chunk_rows - half_low :, :])
    lane_ids = lax.broadcasted_iota(jnp.int32, (half_low, LANES), 1)
    row_ids = lax.broadcasted_iota(jnp.int32, (half_low, LANES), 0)
    counted = lane_ids >= COUNT_LANE
    order = jnp.where(counted, row_ids * (LANES - COUNT_LANE) + lane_ids - COUNT_LANE, devices)
    package = jnp.where(order == me, count, 0.0)
    for at, block in enumerate(blocks):
        value = block * block * count
        value = value if at == 0 else pltpu.roll(value, at * LOW, 1)
        inside = jnp.logical_and(lane_ids >= at * LOW, lane_ids < (at + 1) * LOW)
        package = jnp.where(inside, value, package)
    sums[0] = package

    expected = sum(len(group) for group in partners)
    pl.semaphore_wait(barrier, expected + sends_chosen.astype(jnp.int32) + sends_far.astype(jnp.int32))

    def remote(source, target, pair, device):
        return pltpu.make_async_remote_copy(
            src_ref=source,
            dst_ref=target,
            send_sem=pair.at[0],
            recv_sem=pair.at[1],
            device_id=(device,),
            device_id_type=MESH,
        )

    def stage_copies(stage):
        copies = []
        base = sum(len(group) for group in partners[:stage])
        for at, device in enumerate(partners[stage]):
            copies.append(
                pltpu.make_async_remote_copy(
                    src_ref=sums.at[stage],
                    dst_ref=small.at[base + at],
                    send_sem=small_send.at[base + at],
                    recv_sem=small_recv.at[base + at],
                    device_id=(device,),
                    device_id_type=MESH,
                )
            )
        return copies

    def cross(slot, chunk):
        return remote(cand.at[slot, chunk], cand.at[slot, chunk], cross_sem.at[chunk], partner)

    def relay(slot, chunk):
        return remote(cand.at[slot, chunk], cand.at[slot, chunk], relay_sem.at[chunk], sibling)

    def forward(chunk):
        return remote(chosen.at[chunk], cand.at[TEAM, chunk], chosen_sem.at[chunk], chosen_to)

    to_sibling = remote(cand.at[place], cand.at[place], whole_sem.at[0], sibling)
    from_sibling = remote(cand.at[near], cand.at[near], whole_sem.at[0], sibling)
    to_far = remote(cand.at[place], cand.at[TEAM + 1], whole_sem.at[1], far_to)

    first_stage = stage_copies(0)
    for copy in first_stage:
        copy.start()
    for chunk in range(chunks):
        cross(place, chunk).start()
    to_sibling.start()
    pl.when(sends_far)(to_far.start)
    for fetch in fetches:
        fetch.start()

    def pass_on(chunk):
        cross(across, chunk).wait_recv()
        relay(across, chunk).start()

    stages = [first_stage]
    for stage in range(len(groups)):
        if stage > 0:
            stages.append(stage_copies(stage))
            for copy in stages[stage]:
                copy.start()
        if stage == len(groups) - 1:
            pass_on(0)
        base = sum(len(group) for group in partners[:stage])
        total = sums[stage]
        for at, copy in enumerate(stages[stage]):
            copy.wait_recv()
            total = total + small[base + at]
        sums[stage + 1] = total

    reduced = sums[len(groups)]
    counts = jnp.where(counted, reduced, 0.0)

    def source_place(slot):
        found = jnp.full((1, 1), 1.0, jnp.float32) * (slot - REACH - start).astype(jnp.float32)
        for distance in range(-REACH, REACH):
            ends = jnp.sum(jnp.where(order <= slot + distance, counts, 0.0), keepdims=True)
            found = found + jnp.where(ends <= slot.astype(jnp.float32), 1.0, 0.0)
        return jnp.broadcast_to(found, (chunk_rows, LANES))

    forward_place = source_place(chosen_to)
    from_sibling.wait_recv()

    def team_value(which, chunk):
        value = cand[0, chunk]
        for at in range(1, TEAM):
            value = jnp.where(which == at, cand[at, chunk], value)
        return value

    def send_chosen(chunk):
        relay(both, chunk).wait_recv()
        chosen[chunk] = team_value(forward_place, chunk)
        pl.when(sends_chosen)(forward(chunk).start)

    for chunk in range(1, chunks):
        pass_on(chunk)
        send_chosen(chunk - 1)
    send_chosen(chunks - 1)

    for fetch in fetches:
        fetch.wait()
    work = Work(devices, grid, tables)
    totals = [reduced if at == 0 else pltpu.roll(reduced, LANES - at * LOW, 1) for at in range(2 * PARTS)]
    drift = work.drifts(noise_ref, totals)
    taken = [accept_ref[0, move] == 1 for move in range(len(drift))]
    gains, offsets = work.unrolled(drift, taken)
    offset_states = [work.folded(value) for value in offsets]
    offset_fields = [work.fields(state) for state in offset_states]

    own_place = source_place(me)
    first_side = jnp.broadcast_to(jnp.full((1, 1), 1.0, jnp.float32) * side.astype(jnp.float32), (chunk_rows, LANES)) < 0.5
    before, after = own_place < 0.0, own_place > TEAM - 1.0
    use_chosen = jnp.logical_or(jnp.logical_and(first_side, before), jnp.logical_and(jnp.logical_not(first_side), after))
    use_far = jnp.logical_and(jnp.logical_or(before, after), jnp.logical_not(use_chosen))

    def arrived_far():
        remote(cand.at[TEAM + 1], cand.at[TEAM + 1], whole_sem.at[1], far_from).wait_recv()

    pl.when(takes_far)(arrived_far)
    pieces = []
    for chunk in range(chunks):
        def arrived():
            remote(chosen.at[chunk], cand.at[TEAM, chunk], chosen_sem.at[chunk], chosen_from).wait_recv()

        pl.when(takes_chosen)(arrived)
        value = team_value(own_place, chunk)
        value = jnp.where(use_chosen, cand[TEAM, chunk], value)
        pieces.append(jnp.where(use_far, cand[TEAM + 1, chunk], value))
    present = [jnp.concatenate(pieces[part * per_part : (part + 1) * per_part], axis=0) for part in range(PARTS)]

    moved = present
    for move in range(len(drift)):
        candidate = [work.keep * moved[part] + drift[move][part] for part in range(PARTS)]
        moved = [jnp.where(taken[move], candidate[part], moved[part]) for part in range(PARTS)]
    for part in range(PARTS):
        moved_stage[0, part] = moved[part]
    leave = pltpu.make_async_copy(moved_stage, moved_ref, load_sem)
    leave.start()

    base_state = work.folded(present)
    base_fields = work.fields(base_state)
    states = [gain * base_state + state for gain, state in zip(gains, offset_states)]
    fields = [gain * base_fields + value for gain, value in zip(gains, offset_fields)]
    for move, score in enumerate(work.scores(states, fields, observed_ref)):
        misfit_ref[0, move] = score

    leave.wait()
    for copies in stages:
        for copy in copies:
            copy.wait_send()
    to_sibling.wait_send()
    pl.when(sends_far)(to_far.wait_send)
    for chunk in range(chunks):
        cross(place, chunk).wait_send()
        relay(across, chunk).wait_send()
        pl.when(sends_chosen)(forward(chunk).wait_send)


def halves(table):
    table = np.asarray(table, np.float64)
    high = table.astype(np.float32).astype(ml_dtypes.bfloat16)
    rest = (table - high.astype(np.float64)).astype(np.float32).astype(ml_dtypes.bfloat16)
    return np.stack([high, rest])


def make_tables(grid):
    half = grid // 2
    angle = 2.0 * math.pi / grid
    index = np.arange(grid)
    low = np.arange(half)
    phase = (index[:, None] * low[None, :] % grid) * angle
    sines = np.sin(phase)
    sines[:, 0] = 1.0 - 2.0 * (index % 2)
    fold = np.concatenate([np.cos(phase), sines], axis=1)
    weight = np.where(low == 0, 1.0, 2.0)[:, None]
    back = np.concatenate([weight * np.cos(phase).T, -weight * np.sin(phase).T], axis=0) / spectral_scale
    fore = np.concatenate([np.cos(phase), -np.sin(phase)], axis=1) * (spectral_scale / (grid * grid))
    flip = np.zeros((half, half))
    flip[low, (half - low) % half] = 1.0
    wave_y = np.concatenate([low, np.where(low == 0, half, low)]).astype(np.float64)[:, None]
    wave_x = low.astype(np.float64)[None, :]
    square = wave_y**2 + wave_x**2
    inverse = np.where(square > 0, 1.0 / np.maximum(square, 1.0), 0.0)
    damping = 1.0 / (1.0 + time_step * viscosity * square)
    keeper = (np.abs(wave_y) <= grid // 3) & (wave_x <= grid // 3)
    doubled = np.where(np.concatenate([low, low])[:, None] == 0, 1.0, 2.0)
    flux = -time_step * keeper * doubled * damping
    signed = np.where(index < half, index, index - grid).astype(np.float64)[:, None]
    prior = prior_amplitude / (1.0 + np.sqrt(signed**2 + wave_x**2) / 8.0)
    scales = np.stack([inverse, damping, flux, step_size * prior]).astype(np.float32)
    return (
        halves(fold), halves(fold.T), halves(back), halves(fore),
        flip.astype(ml_dtypes.bfloat16), scales,
    )


def split(value):
    high = value.astype(jnp.bfloat16)
    return high, (value - high.astype(jnp.float32)).astype(jnp.bfloat16)


def dot(a, b):
    return jnp.dot(a, b, preferred_element_type=jnp.float32)


def table_left(table, value):
    high, rest = split(value)
    return dot(table[0], high) + dot(table[0], rest) + dot(table[1], high)


def table_right(value, table):
    high, rest = split(value)
    return dot(high, table[0]) + dot(rest, table[0]) + dot(high, table[1])


class Work:
    def __init__(self, devices, grid, tables):
        fold, unfold, back, fore, flip, scales = tables
        self.devices, self.grid, self.half = devices, grid, grid // 2
        self.fold = (fold[0], fold[1])
        self.unfold = (unfold[0], unfold[1])
        self.back = (back[0], back[1])
        self.fore = (fore[0], fore[1])
        self.flip = flip[...]
        self.scales = scales
        self.keep = math.sqrt(1.0 - step_size * step_size)
        row_ids = lax.broadcasted_iota(jnp.int32, (self.half, grid), 0)
        self.first = row_ids == 0
        self.wave = row_ids.astype(jnp.float32)
        self.wave_x = lax.broadcasted_iota(jnp.int32, (grid, self.half), 1).astype(jnp.float32)

    def wide(self, index):
        value = self.scales[index]
        return jnp.concatenate([value, value], axis=1)

    def turn(self, value):
        return jnp.concatenate([-value[:, self.half :], value[:, : self.half]], axis=1)

    def drifts(self, noise_ref, totals):
        half_low = LOW // 2
        lanes = lax.broadcasted_iota(jnp.int32, (half_low, self.half), 1)
        prior = self.scales[3]
        inner = slice(half_low, self.grid - half_low)
        spreads = []
        for part in range(PARTS):
            head, tail = [
                step_size * jnp.sqrt(total * (1.0 / self.devices) + 1e-06)
                for total in totals[2 * part : 2 * part + 2]
            ]
            top = jnp.where(lanes < LOW, head, prior[:half_low])
            bottom = jnp.where(lanes < LOW, tail, prior[self.grid - half_low :])
            spreads.append(jnp.concatenate([top, prior[inner], bottom], axis=0))
        return [
            [spreads[part] * noise_ref[move, 0, part] for part in range(PARTS)]
            for move in range(noise_ref.shape[0])
        ]

    def unrolled(self, drift, taken):
        gain, offset = 1.0, [jnp.zeros_like(value) for value in drift[0]]
        gains, offsets = [], []
        for step, accepted in zip(drift, taken):
            new_gain = self.keep * gain
            new_offset = [self.keep * old + value for old, value in zip(offset, step)]
            gains.append(new_gain)
            offsets.append(new_offset)
            gain = jnp.where(accepted, new_gain, gain)
            offset = [jnp.where(accepted, new, old) for new, old in zip(new_offset, offset)]
        return gains, offsets

    def folded(self, parts):
        half = self.half
        top = jnp.concatenate([part[:half] for part in parts], axis=1)
        high, rest = split(jnp.concatenate([part[half:] for part in parts], axis=1))
        other = dot(self.flip, high) + dot(self.flip, rest)
        even = top + jnp.where(self.first, 0.0, other)
        odd = jnp.where(self.first, other, self.turn(top - other))
        return jnp.concatenate([even, odd], axis=0)

    def fields(self, state):
        half, wave_x = self.half, self.wave_x
        psi = state * self.wide(0)
        even, odd = psi[:half], psi[half:]
        along_y = jnp.concatenate(
            [self.wave * odd, jnp.where(self.first, -float(half) * self.turn(odd), -self.wave * even)], axis=0
        )
        along_x = jnp.concatenate([wave_x * psi[:, half:], -wave_x * psi[:, :half]], axis=1)
        rows = [table_left(self.fold, value) for value in (state, along_y, along_x)]
        return table_right(jnp.concatenate(rows, axis=0), self.back)

    def scores(self, states, fields, observed_ref):
        grid, half, wave, wave_x = self.grid, self.half, self.wave, self.wave_x
        products = []
        for value in fields:
            vort = value[:grid]
            products += [value[grid : 2 * grid] * vort, value[2 * grid :] * vort]
        rows = table_right(jnp.concatenate(products, axis=0), self.fore)
        damping, flux_scale = self.wide(1), self.wide(2)
        finals = []
        for move, state in enumerate(states):
            flux_u = table_left(self.unfold, rows[(2 * move) * grid : (2 * move + 1) * grid])
            flux_v = table_left(self.unfold, rows[(2 * move + 1) * grid : (2 * move + 2) * grid])
            along_x = jnp.concatenate([-wave_x * flux_u[:, half:], wave_x * flux_u[:, :half]], axis=1)
            along_y = jnp.concatenate([wave * flux_v[half:], -wave * flux_v[:half]], axis=0)
            finals.append(table_left(self.fold, state * damping + flux_scale * (along_x + along_y)))
        forecast = table_right(jnp.concatenate(finals, axis=0), self.back)
        scale = 1.0 / (2.0 * noise_level * noise_level * grid * grid)
        result = []
        for move in range(len(states)):
            gap = forecast[move * grid : (move + 1) * grid] - observed_ref[...]
            result.append(jnp.sum(gap * gap) * scale)
        return result


def body(devices, particles, offspring, noise, accept, observed):
    groups = split_bits(devices)
    _, _, grid, half = particles.shape
    moves = noise.shape[0]
    assert particles.shape[0] == 1 and half == LANES and devices <= LOW // 2 * (LANES - COUNT_LANE)
    copies = sum((1 << width) - 1 for _, width in groups)
    package = LOW // 2
    assert 2 * PARTS * LOW == COUNT_LANE
    slots = TEAM + 2
    assert devices % TEAM == 0 and (PARTS * grid) % CHUNKS == 0
    chunk_shape = (CHUNKS, PARTS * grid // CHUNKS, half)
    tables = [jnp.asarray(table) for table in make_tables(grid)]
    hbm = pl.BlockSpec(memory_space=HBM)
    smem = pl.BlockSpec(memory_space=pltpu.SMEM)
    fetched = [noise, observed] + tables
    moved, misfit = pl.pallas_call(
        functools.partial(filter_kernel, devices, groups),
        out_shape=(
            jax.ShapeDtypeStruct((1, PARTS, grid, half), jnp.float32),
            jax.ShapeDtypeStruct((1, moves), jnp.float32),
        ),
        in_specs=[hbm, smem, smem] + [hbm] * len(fetched),
        out_specs=(hbm, smem),
        scratch_shapes=[
            pltpu.VMEM((slots,) + chunk_shape, jnp.float32),
            pltpu.VMEM(chunk_shape, jnp.float32),
            pltpu.VMEM((len(groups) + 1, package, LANES), jnp.float32),
            pltpu.VMEM((copies, package, LANES), jnp.float32),
            pltpu.VMEM((1, PARTS, grid, half), jnp.float32),
        ]
        + [pltpu.VMEM(value.shape, value.dtype) for value in fetched]
        + [
            pltpu.SemaphoreType.DMA,
            pltpu.SemaphoreType.DMA((2, 2)),
            pltpu.SemaphoreType.DMA((CHUNKS, 2)),
            pltpu.SemaphoreType.DMA((CHUNKS, 2)),
            pltpu.SemaphoreType.DMA((CHUNKS, 2)),
            pltpu.SemaphoreType.DMA((copies,)),
            pltpu.SemaphoreType.DMA((copies,)),
            pltpu.SemaphoreType.DMA((len(fetched),)),
        ],
        compiler_params=pltpu.CompilerParams(
            collective_id=0, has_side_effects=True, vmem_limit_bytes=63 * 1024 * 1024
        ),
        name="filter",
    )(particles.reshape(chunk_shape), offspring, accept.T, *fetched)
    return moved, misfit.T


def solution(mesh):
    return jax.shard_map(
        functools.partial(body, mesh.shape["dom"]),
        mesh=mesh,
        in_specs=(
            P("dom", None, None, None),
            P("dom"),
            P(None, "dom", None, None, None),
            P(None, "dom"),
            P(),
        ),
        out_specs=(P("dom", None, None, None), P(None, "dom")),
        check_vma=False,
    )
```

```python
import functools
import math

import jax
import jax.numpy as jnp
import ml_dtypes
import numpy as np
from jax import lax
from jax.experimental import pallas as pl
from jax.experimental.pallas import tpu as pltpu
from jax.sharding import PartitionSpec as P

REACH = 3
LOW = 16
LANES = 128
COUNT_LANE = 64
PARTS = 2
GROUP_BITS = 3
TEAM = 4
CHUNKS = 4
AHEAD = 2

time_step = 0.05
viscosity = 0.001
noise_level = 0.5
spectral_scale = 64.0
prior_amplitude = 1.5
step_size = 0.4

MESH = pl.DeviceIdType.MESH
HBM = pltpu.MemorySpace.HBM


def split_bits(devices):
    bits = devices.bit_length() - 1
    assert 1 << bits == devices
    groups = []
    first = 0
    while first < bits:
        width = min(GROUP_BITS, bits - first)
        groups.append((first, width))
        first += width
    return groups


def filter_kernel(
    devices, groups, x_ref, count_ref, accept_ref, noise_hbm, observed_hbm, *rest
):
    tables_hbm = rest[:6]
    moved_ref, misfit_ref = rest[6:8]
    cand, chosen, sums, small, moved_stage, noise_ref, observed_ref = rest[8:15]
    tables = rest[15:21]
    load_sem, whole_sem, cross_sem, relay_sem, chosen_sem, small_send, small_recv, fetch_sem = rest[21:]
    chunks, chunk_rows, _ = x_ref.shape
    grid = chunks * chunk_rows // PARTS
    me = lax.axis_index("dom")
    place = lax.rem(me, TEAM)
    start = me - place
    core = lax.rem(place, 2)
    side = place // 2
    near = place + 1 - 2 * core
    across = lax.rem(place + 2, TEAM)
    both = lax.rem(near + 2, TEAM)
    sibling, partner = start + near, start + across
    chosen_to = me + TEAM - 2 * TEAM * side
    chosen_from = me - TEAM + 2 * TEAM * side
    sends_chosen = jnp.logical_and(chosen_to >= 0, chosen_to < devices)
    takes_chosen = jnp.logical_and(chosen_from >= 0, chosen_from < devices)
    far_to = jnp.where(place == 0, me - REACH, me + REACH)
    far_from = jnp.where(place == 1, me + REACH, me - REACH)
    outer = jnp.logical_or(place == 0, place == TEAM - 1)
    sends_far = jnp.logical_and(outer, jnp.logical_and(far_to >= 0, far_to < devices))
    takes_far = jnp.logical_and(
        jnp.logical_not(outer), jnp.logical_and(far_from >= 0, far_from < devices)
    )

    load = pltpu.make_async_copy(x_ref, cand.at[place], load_sem)
    load.start()
    fetches = [
        pltpu.make_async_copy(source, target, fetch_sem.at[at])
        for at, (source, target) in enumerate(
            zip((noise_hbm, observed_hbm) + tables_hbm, (noise_ref, observed_ref) + tables)
        )
    ]
    barrier = pltpu.get_barrier_semaphore()

    def greet(device):
        pl.semaphore_signal(barrier, inc=1, device_id=(device,), device_id_type=MESH)

    partners = []
    for first, width in groups:
        partners.append([jnp.bitwise_xor(me, k << first) for k in range(1, 1 << width)])
    for group in partners:
        for device in group:
            greet(device)
    pl.when(takes_chosen)(lambda: greet(chosen_from))
    pl.when(takes_far)(lambda: greet(far_from))

    load.wait()
    count = count_ref[0].astype(jnp.float32)
    half_low = LOW // 2
    per_part = chunks // PARTS
    blocks = []
    for part in range(PARTS):
        blocks.append(cand[place, part * per_part, :half_low, :])
        blocks.append(cand[place, (part + 1) * per_part - 1, chunk_rows - half_low :, :])
    lane_ids = lax.broadcasted_iota(jnp.int32, (half_low, LANES), 1)
    row_ids = lax.broadcasted_iota(jnp.int32, (half_low, LANES), 0)
    counted = lane_ids >= COUNT_LANE
    order = jnp.where(counted, row_ids * (LANES - COUNT_LANE) + lane_ids - COUNT_LANE, devices)
    package = jnp.where(order == me, count, 0.0)
    for at, block in enumerate(blocks):
        value = block * block * count
        value = value if at == 0 else pltpu.roll(value, at * LOW, 1)
        inside = jnp.logical_and(lane_ids >= at * LOW, lane_ids < (at + 1) * LOW)
        package = jnp.where(inside, value, package)
    sums[0] = package

    expected = sum(len(group) for group in partners)
    pl.semaphore_wait(barrier, expected + sends_chosen.astype(jnp.int32) + sends_far.astype(jnp.int32))

    def remote(source, target, pair, device):
        return pltpu.make_async_remote_copy(
            src_ref=source,
            dst_ref=target,
            send_sem=pair.at[0],
            recv_sem=pair.at[1],
            device_id=(device,),
            device_id_type=MESH,
        )

    def stage_copies(stage):
        copies = []
        base = sum(len(group) for group in partners[:stage])
        for at, device in enumerate(partners[stage]):
            copies.append(
                pltpu.make_async_remote_copy(
                    src_ref=sums.at[stage],
                    dst_ref=small.at[base + at],
                    send_sem=small_send.at[base + at],
                    recv_sem=small_recv.at[base + at],
                    device_id=(device,),
                    device_id_type=MESH,
                )
            )
        return copies

    def cross(slot, chunk):
        return remote(cand.at[slot, chunk], cand.at[slot, chunk], cross_sem.at[chunk], partner)

    def relay(slot, chunk):
        return remote(cand.at[slot, chunk], cand.at[slot, chunk], relay_sem.at[chunk], sibling)

    def forward(chunk):
        return remote(chosen.at[chunk], cand.at[TEAM, chunk], chosen_sem.at[chunk], chosen_to)

    to_sibling = remote(cand.at[place], cand.at[place], whole_sem.at[0], sibling)
    from_sibling = remote(cand.at[near], cand.at[near], whole_sem.at[0], sibling)
    to_far = remote(cand.at[place], cand.at[TEAM + 1], whole_sem.at[1], far_to)

    first_stage = stage_copies(0)
    for copy in first_stage:
        copy.start()
    for chunk in range(AHEAD):
        cross(place, chunk).start()
    to_sibling.start()
    pl.when(sends_far)(to_far.start)
    for fetch in fetches:
        fetch.start()

    def pass_on(chunk):
        cross(across, chunk).wait_recv()
        if chunk + AHEAD < chunks:
            cross(place, chunk + AHEAD).start()
        relay(across, chunk).start()

    stages = [first_stage]
    for stage in range(len(groups)):
        if stage > 0:
            stages.append(stage_copies(stage))
            for copy in stages[stage]:
                copy.start()
        if stage == len(groups) - 1:
            pass_on(0)
        base = sum(len(group) for group in partners[:stage])
        total = sums[stage]
        for at, copy in enumerate(stages[stage]):
            copy.wait_recv()
            total = total + small[base + at]
        sums[stage + 1] = total

    reduced = sums[len(groups)]
    counts = jnp.where(counted, reduced, 0.0)

    def source_place(slot):
        found = jnp.full((1, 1), 1.0, jnp.float32) * (slot - REACH - start).astype(jnp.float32)
        for distance in range(-REACH, REACH):
            ends = jnp.sum(jnp.where(order <= slot + distance, counts, 0.0), keepdims=True)
            found = found + jnp.where(ends <= slot.astype(jnp.float32), 1.0, 0.0)
        return jnp.broadcast_to(found, (chunk_rows, LANES))

    forward_place = source_place(chosen_to)
    from_sibling.wait_recv()

    def team_value(which, chunk):
        value = cand[0, chunk]
        for at in range(1, TEAM):
            value = jnp.where(which == at, cand[at, chunk], value)
        return value

    def send_chosen(chunk):
        relay(both, chunk).wait_recv()
        chosen[chunk] = team_value(forward_place, chunk)
        pl.when(sends_chosen)(forward(chunk).start)

    for chunk in range(1, chunks):
        pass_on(chunk)
        send_chosen(chunk - 1)
    send_chosen(chunks - 1)

    for fetch in fetches:
        fetch.wait()
    work = Work(devices, grid, tables)
    totals = [reduced if at == 0 else pltpu.roll(reduced, LANES - at * LOW, 1) for at in range(2 * PARTS)]
    drift = work.drifts(noise_ref, totals)
    taken = [accept_ref[0, move] == 1 for move in range(len(drift))]
    gains, offsets = work.unrolled(drift, taken)
    offset_states = [work.folded(value) for value in offsets]
    offset_fields = [work.fields(state) for state in offset_states]

    own_place = source_place(me)
    first_side = jnp.broadcast_to(jnp.full((1, 1), 1.0, jnp.float32) * side.astype(jnp.float32), (chunk_rows, LANES)) < 0.5
    before, after = own_place < 0.0, own_place > TEAM - 1.0
    use_chosen = jnp.logical_or(jnp.logical_and(first_side, before), jnp.logical_and(jnp.logical_not(first_side), after))
    use_far = jnp.logical_and(jnp.logical_or(before, after), jnp.logical_not(use_chosen))

    def arrived_far():
        remote(cand.at[TEAM + 1], cand.at[TEAM + 1], whole_sem.at[1], far_from).wait_recv()

    pl.when(takes_far)(arrived_far)
    pieces = []
    for chunk in range(chunks):
        def arrived():
            remote(chosen.at[chunk], cand.at[TEAM, chunk], chosen_sem.at[chunk], chosen_from).wait_recv()

        pl.when(takes_chosen)(arrived)
        value = team_value(own_place, chunk)
        value = jnp.where(use_chosen, cand[TEAM, chunk], value)
        pieces.append(jnp.where(use_far, cand[TEAM + 1, chunk], value))
    present = [jnp.concatenate(pieces[part * per_part : (part + 1) * per_part], axis=0) for part in range(PARTS)]

    moved = present
    for move in range(len(drift)):
        candidate = [work.keep * moved[part] + drift[move][part] for part in range(PARTS)]
        moved = [jnp.where(taken[move], candidate[part], moved[part]) for part in range(PARTS)]
    for part in range(PARTS):
        moved_stage[0, part] = moved[part]
    leave = pltpu.make_async_copy(moved_stage, moved_ref, load_sem)
    leave.start()

    base_state = work.folded(present)
    base_fields = work.fields(base_state)
    states = [gain * base_state + state for gain, state in zip(gains, offset_states)]
    fields = [gain * base_fields + value for gain, value in zip(gains, offset_fields)]
    for move, score in enumerate(work.scores(states, fields, observed_ref)):
        misfit_ref[0, move] = score

    leave.wait()
    for copies in stages:
        for copy in copies:
            copy.wait_send()
    to_sibling.wait_send()
    pl.when(sends_far)(to_far.wait_send)
    for chunk in range(chunks):
        cross(place, chunk).wait_send()
        relay(across, chunk).wait_send()
        pl.when(sends_chosen)(forward(chunk).wait_send)


def halves(table):
    table = np.asarray(table, np.float64)
    high = table.astype(np.float32).astype(ml_dtypes.bfloat16)
    rest = (table - high.astype(np.float64)).astype(np.float32).astype(ml_dtypes.bfloat16)
    return np.stack([high, rest])


def make_tables(grid):
    half = grid // 2
    angle = 2.0 * math.pi / grid
    index = np.arange(grid)
    low = np.arange(half)
    phase = (index[:, None] * low[None, :] % grid) * angle
    sines = np.sin(phase)
    sines[:, 0] = 1.0 - 2.0 * (index % 2)
    fold = np.concatenate([np.cos(phase), sines], axis=1)
    weight = np.where(low == 0, 1.0, 2.0)[:, None]
    back = np.concatenate([weight * np.cos(phase).T, -weight * np.sin(phase).T], axis=0) / spectral_scale
    fore = np.concatenate([np.cos(phase), -np.sin(phase)], axis=1) * (spectral_scale / (grid * grid))
    flip = np.zeros((half, half))
    flip[low, (half - low) % half] = 1.0
    wave_y = np.concatenate([low, np.where(low == 0, half, low)]).astype(np.float64)[:, None]
    wave_x = low.astype(np.float64)[None, :]
    square = wave_y**2 + wave_x**2
    inverse = np.where(square > 0, 1.0 / np.maximum(square, 1.0), 0.0)
    damping = 1.0 / (1.0 + time_step * viscosity * square)
    keeper = (np.abs(wave_y) <= grid // 3) & (wave_x <= grid // 3)
    doubled = np.where(np.concatenate([low, low])[:, None] == 0, 1.0, 2.0)
    flux = -time_step * keeper * doubled * damping
    signed = np.where(index < half, index, index - grid).astype(np.float64)[:, None]
    prior = prior_amplitude / (1.0 + np.sqrt(signed**2 + wave_x**2) / 8.0)
    scales = np.stack([inverse, damping, flux, step_size * prior]).astype(np.float32)
    return (
        halves(fold), halves(fold.T), halves(back), halves(fore),
        flip.astype(ml_dtypes.bfloat16), scales,
    )


def split(value):
    high = value.astype(jnp.bfloat16)
    return high, (value - high.astype(jnp.float32)).astype(jnp.bfloat16)


def dot(a, b):
    return jnp.dot(a, b, preferred_element_type=jnp.float32)


def table_left(table, value):
    high, rest = split(value)
    return dot(table[0], high) + dot(table[0], rest) + dot(table[1], high)


def table_right(value, table):
    high, rest = split(value)
    return dot(high, table[0]) + dot(rest, table[0]) + dot(high, table[1])


class Work:
    def __init__(self, devices, grid, tables):
        fold, unfold, back, fore, flip, scales = tables
        self.devices, self.grid, self.half = devices, grid, grid // 2
        self.fold = (fold[0], fold[1])
        self.unfold = (unfold[0], unfold[1])
        self.back = (back[0], back[1])
        self.fore = (fore[0], fore[1])
        self.flip = flip[...]
        self.scales = scales
        self.keep = math.sqrt(1.0 - step_size * step_size)
        row_ids = lax.broadcasted_iota(jnp.int32, (self.half, grid), 0)
        self.first = row_ids == 0
        self.wave = row_ids.astype(jnp.float32)
        self.wave_x = lax.broadcasted_iota(jnp.int32, (grid, self.half), 1).astype(jnp.float32)

    def wide(self, index):
        value = self.scales[index]
        return jnp.concatenate([value, value], axis=1)

    def turn(self, value):
        return jnp.concatenate([-value[:, self.half :], value[:, : self.half]], axis=1)

    def drifts(self, noise_ref, totals):
        half_low = LOW // 2
        lanes = lax.broadcasted_iota(jnp.int32, (half_low, self.half), 1)
        prior = self.scales[3]
        inner = slice(half_low, self.grid - half_low)
        spreads = []
        for part in range(PARTS):
            head, tail = [
                step_size * jnp.sqrt(total * (1.0 / self.devices) + 1e-06)
                for total in totals[2 * part : 2 * part + 2]
            ]
            top = jnp.where(lanes < LOW, head, prior[:half_low])
            bottom = jnp.where(lanes < LOW, tail, prior[self.grid - half_low :])
            spreads.append(jnp.concatenate([top, prior[inner], bottom], axis=0))
        return [
            [spreads[part] * noise_ref[move, 0, part] for part in range(PARTS)]
            for move in range(noise_ref.shape[0])
        ]

    def unrolled(self, drift, taken):
        gain, offset = 1.0, [jnp.zeros_like(value) for value in drift[0]]
        gains, offsets = [], []
        for step, accepted in zip(drift, taken):
            new_gain = self.keep * gain
            new_offset = [self.keep * old + value for old, value in zip(offset, step)]
            gains.append(new_gain)
            offsets.append(new_offset)
            gain = jnp.where(accepted, new_gain, gain)
            offset = [jnp.where(accepted, new, old) for new, old in zip(new_offset, offset)]
        return gains, offsets

    def folded(self, parts):
        half = self.half
        top = jnp.concatenate([part[:half] for part in parts], axis=1)
        high, rest = split(jnp.concatenate([part[half:] for part in parts], axis=1))
        other = dot(self.flip, high) + dot(self.flip, rest)
        even = top + jnp.where(self.first, 0.0, other)
        odd = jnp.where(self.first, other, self.turn(top - other))
        return jnp.concatenate([even, odd], axis=0)

    def fields(self, state):
        half, wave_x = self.half, self.wave_x
        psi = state * self.wide(0)
        even, odd = psi[:half], psi[half:]
        along_y = jnp.concatenate(
            [self.wave * odd, jnp.where(self.first, -float(half) * self.turn(odd), -self.wave * even)], axis=0
        )
        along_x = jnp.concatenate([wave_x * psi[:, half:], -wave_x * psi[:, :half]], axis=1)
        rows = [table_left(self.fold, value) for value in (state, along_y, along_x)]
        return table_right(jnp.concatenate(rows, axis=0), self.back)

    def scores(self, states, fields, observed_ref):
        grid, half, wave, wave_x = self.grid, self.half, self.wave, self.wave_x
        products = []
        for value in fields:
            vort = value[:grid]
            products += [value[grid : 2 * grid] * vort, value[2 * grid :] * vort]
        rows = table_right(jnp.concatenate(products, axis=0), self.fore)
        damping, flux_scale = self.wide(1), self.wide(2)
        finals = []
        for move, state in enumerate(states):
            flux_u = table_left(self.unfold, rows[(2 * move) * grid : (2 * move + 1) * grid])
            flux_v = table_left(self.unfold, rows[(2 * move + 1) * grid : (2 * move + 2) * grid])
            along_x = jnp.concatenate([-wave_x * flux_u[:, half:], wave_x * flux_u[:, :half]], axis=1)
            along_y = jnp.concatenate([wave * flux_v[half:], -wave * flux_v[:half]], axis=0)
            finals.append(table_left(self.fold, state * damping + flux_scale * (along_x + along_y)))
        forecast = table_right(jnp.concatenate(finals, axis=0), self.back)
        scale = 1.0 / (2.0 * noise_level * noise_level * grid * grid)
        result = []
        for move in range(len(states)):
            gap = forecast[move * grid : (move + 1) * grid] - observed_ref[...]
            result.append(jnp.sum(gap * gap) * scale)
        return result


def body(devices, particles, offspring, noise, accept, observed):
    groups = split_bits(devices)
    _, _, grid, half = particles.shape
    moves = noise.shape[0]
    assert particles.shape[0] == 1 and half == LANES and devices <= LOW // 2 * (LANES - COUNT_LANE)
    copies = sum((1 << width) - 1 for _, width in groups)
    package = LOW // 2
    assert 2 * PARTS * LOW == COUNT_LANE
    slots = TEAM + 2
    assert devices % TEAM == 0 and (PARTS * grid) % CHUNKS == 0
    chunk_shape = (CHUNKS, PARTS * grid // CHUNKS, half)
    tables = [jnp.asarray(table) for table in make_tables(grid)]
    hbm = pl.BlockSpec(memory_space=HBM)
    smem = pl.BlockSpec(memory_space=pltpu.SMEM)
    fetched = [noise, observed] + tables
    moved, misfit = pl.pallas_call(
        functools.partial(filter_kernel, devices, groups),
        out_shape=(
            jax.ShapeDtypeStruct((1, PARTS, grid, half), jnp.float32),
            jax.ShapeDtypeStruct((1, moves), jnp.float32),
        ),
        in_specs=[hbm, smem, smem] + [hbm] * len(fetched),
        out_specs=(hbm, smem),
        scratch_shapes=[
            pltpu.VMEM((slots,) + chunk_shape, jnp.float32),
            pltpu.VMEM(chunk_shape, jnp.float32),
            pltpu.VMEM((len(groups) + 1, package, LANES), jnp.float32),
            pltpu.VMEM((copies, package, LANES), jnp.float32),
            pltpu.VMEM((1, PARTS, grid, half), jnp.float32),
        ]
        + [pltpu.VMEM(value.shape, value.dtype) for value in fetched]
        + [
            pltpu.SemaphoreType.DMA,
            pltpu.SemaphoreType.DMA((2, 2)),
            pltpu.SemaphoreType.DMA((CHUNKS, 2)),
            pltpu.SemaphoreType.DMA((CHUNKS, 2)),
            pltpu.SemaphoreType.DMA((CHUNKS, 2)),
            pltpu.SemaphoreType.DMA((copies,)),
            pltpu.SemaphoreType.DMA((copies,)),
            pltpu.SemaphoreType.DMA((len(fetched),)),
        ],
        compiler_params=pltpu.CompilerParams(
            collective_id=0, has_side_effects=True, vmem_limit_bytes=63 * 1024 * 1024
        ),
        name="filter",
    )(particles.reshape(chunk_shape), offspring, accept.T, *fetched)
    return moved, misfit.T


def solution(mesh):
    return jax.shard_map(
        functools.partial(body, mesh.shape["dom"]),
        mesh=mesh,
        in_specs=(
            P("dom", None, None, None),
            P("dom"),
            P(None, "dom", None, None, None),
            P(None, "dom"),
            P(),
        ),
        out_specs=(P("dom", None, None, None), P(None, "dom")),
        check_vma=False,
    )
```

```python
import functools
import math

import jax
import jax.numpy as jnp
import ml_dtypes
import numpy as np
from jax import lax
from jax.experimental import pallas as pl
from jax.experimental.pallas import tpu as pltpu
from jax.sharding import PartitionSpec as P

REACH = 3
LOW = 16
LANES = 128
COUNT_LANE = 64
PARTS = 2
GROUP_BITS = 3
TEAM = 4
CHUNKS = 2

time_step = 0.05
viscosity = 0.001
noise_level = 0.5
spectral_scale = 64.0
prior_amplitude = 1.5
step_size = 0.4

MESH = pl.DeviceIdType.MESH
HBM = pltpu.MemorySpace.HBM


def split_bits(devices):
    bits = devices.bit_length() - 1
    assert 1 << bits == devices
    groups = []
    first = 0
    while first < bits:
        width = min(GROUP_BITS, bits - first)
        groups.append((first, width))
        first += width
    return groups


def filter_kernel(
    devices, groups, x_ref, count_ref, accept_ref, noise_hbm, observed_hbm, *rest
):
    tables_hbm = rest[:6]
    moved_ref, misfit_ref = rest[6:8]
    cand, chosen, sums, small, moved_stage, noise_ref, observed_ref = rest[8:15]
    tables = rest[15:21]
    load_sem, whole_sem, cross_sem, relay_sem, chosen_sem, small_send, small_recv, fetch_sem = rest[21:]
    chunks, chunk_rows, _ = x_ref.shape
    grid = chunks * chunk_rows // PARTS
    me = lax.axis_index("dom")
    place = lax.rem(me, TEAM)
    start = me - place
    core = lax.rem(place, 2)
    side = place // 2
    near = place + 1 - 2 * core
    across = lax.rem(place + 2, TEAM)
    both = lax.rem(near + 2, TEAM)
    sibling, partner = start + near, start + across
    chosen_to = me + TEAM - 2 * TEAM * side
    chosen_from = me - TEAM + 2 * TEAM * side
    sends_chosen = jnp.logical_and(chosen_to >= 0, chosen_to < devices)
    takes_chosen = jnp.logical_and(chosen_from >= 0, chosen_from < devices)
    far_to = jnp.where(place == 0, me - REACH, me + REACH)
    far_from = jnp.where(place == 1, me + REACH, me - REACH)
    outer = jnp.logical_or(place == 0, place == TEAM - 1)
    sends_far = jnp.logical_and(outer, jnp.logical_and(far_to >= 0, far_to < devices))
    takes_far = jnp.logical_and(
        jnp.logical_not(outer), jnp.logical_and(far_from >= 0, far_from < devices)
    )

    load = pltpu.make_async_copy(x_ref, cand.at[place], load_sem)
    load.start()
    fetches = [
        pltpu.make_async_copy(source, target, fetch_sem.at[at])
        for at, (source, target) in enumerate(
            zip((noise_hbm, observed_hbm) + tables_hbm, (noise_ref, observed_ref) + tables)
        )
    ]
    barrier = pltpu.get_barrier_semaphore()

    def greet(device):
        pl.semaphore_signal(barrier, inc=1, device_id=(device,), device_id_type=MESH)

    partners = []
    for first, width in groups:
        partners.append([jnp.bitwise_xor(me, k << first) for k in range(1, 1 << width)])
    for group in partners:
        for device in group:
            greet(device)
    pl.when(takes_chosen)(lambda: greet(chosen_from))
    pl.when(takes_far)(lambda: greet(far_from))

    load.wait()
    count = count_ref[0].astype(jnp.float32)
    half_low = LOW // 2
    per_part = chunks // PARTS
    blocks = []
    for part in range(PARTS):
        blocks.append(cand[place, part * per_part, :half_low, :])
        blocks.append(cand[place, (part + 1) * per_part - 1, chunk_rows - half_low :, :])
    lane_ids = lax.broadcasted_iota(jnp.int32, (half_low, LANES), 1)
    row_ids = lax.broadcasted_iota(jnp.int32, (half_low, LANES), 0)
    counted = lane_ids >= COUNT_LANE
    order = jnp.where(counted, row_ids * (LANES - COUNT_LANE) + lane_ids - COUNT_LANE, devices)
    package = jnp.where(order == me, count, 0.0)
    for at, block in enumerate(blocks):
        value = block * block * count
        value = value if at == 0 else pltpu.roll(value, at * LOW, 1)
        inside = jnp.logical_and(lane_ids >= at * LOW, lane_ids < (at + 1) * LOW)
        package = jnp.where(inside, value, package)
    sums[0] = package

    expected = sum(len(group) for group in partners)
    pl.semaphore_wait(barrier, expected + sends_chosen.astype(jnp.int32) + sends_far.astype(jnp.int32))

    def remote(source, target, pair, device):
        return pltpu.make_async_remote_copy(
            src_ref=source,
            dst_ref=target,
            send_sem=pair.at[0],
            recv_sem=pair.at[1],
            device_id=(device,),
            device_id_type=MESH,
        )

    def stage_copies(stage):
        copies = []
        base = sum(len(group) for group in partners[:stage])
        for at, device in enumerate(partners[stage]):
            copies.append(
                pltpu.make_async_remote_copy(
                    src_ref=sums.at[stage],
                    dst_ref=small.at[base + at],
                    send_sem=small_send.at[base + at],
                    recv_sem=small_recv.at[base + at],
                    device_id=(device,),
                    device_id_type=MESH,
                )
            )
        return copies

    def cross(slot, chunk):
        return remote(cand.at[slot, chunk], cand.at[slot, chunk], cross_sem.at[chunk], partner)

    def relay(slot, chunk):
        return remote(cand.at[slot, chunk], cand.at[slot, chunk], relay_sem.at[chunk], sibling)

    def forward(chunk):
        return remote(chosen.at[chunk], cand.at[TEAM, chunk], chosen_sem.at[chunk], chosen_to)

    to_sibling = remote(cand.at[place], cand.at[place], whole_sem.at[0], sibling)
    from_sibling = remote(cand.at[near], cand.at[near], whole_sem.at[0], sibling)
    to_far = remote(cand.at[place], cand.at[TEAM + 1], whole_sem.at[1], far_to)

    first_stage = stage_copies(0)
    for copy in first_stage:
        copy.start()
    for chunk in range(chunks):
        cross(place, chunk).start()
    to_sibling.start()
    pl.when(sends_far)(to_far.start)
    for fetch in fetches:
        fetch.start()

    def pass_on(chunk):
        cross(across, chunk).wait_recv()
        relay(across, chunk).start()

    stages = [first_stage]
    for stage in range(len(groups)):
        if stage > 0:
            stages.append(stage_copies(stage))
            for copy in stages[stage]:
                copy.start()
        if stage == len(groups) - 1:
            pass_on(0)
        base = sum(len(group) for group in partners[:stage])
        total = sums[stage]
        for at, copy in enumerate(stages[stage]):
            copy.wait_recv()
            total = total + small[base + at]
        sums[stage + 1] = total

    reduced = sums[len(groups)]
    counts = jnp.where(counted, reduced, 0.0)

    def source_place(slot):
        found = jnp.full((1, 1), 1.0, jnp.float32) * (slot - REACH - start).astype(jnp.float32)
        for distance in range(-REACH, REACH):
            ends = jnp.sum(jnp.where(order <= slot + distance, counts, 0.0), keepdims=True)
            found = found + jnp.where(ends <= slot.astype(jnp.float32), 1.0, 0.0)
        return jnp.broadcast_to(found, (chunk_rows, LANES))

    forward_place = source_place(chosen_to)
    from_sibling.wait_recv()

    def team_value(which, chunk):
        value = cand[0, chunk]
        for at in range(1, TEAM):
            value = jnp.where(which == at, cand[at, chunk], value)
        return value

    def send_chosen(chunk):
        relay(both, chunk).wait_recv()
        chosen[chunk] = team_value(forward_place, chunk)
        pl.when(sends_chosen)(forward(chunk).start)

    for chunk in range(1, chunks):
        pass_on(chunk)
        send_chosen(chunk - 1)
    send_chosen(chunks - 1)

    for fetch in fetches:
        fetch.wait()
    work = Work(devices, grid, tables)
    totals = [reduced if at == 0 else pltpu.roll(reduced, LANES - at * LOW, 1) for at in range(2 * PARTS)]
    drift = work.drifts(noise_ref, totals)
    taken = [accept_ref[0, move] == 1 for move in range(len(drift))]
    gains, offsets = work.unrolled(drift, taken)
    offset_states = [work.folded(value) for value in offsets]
    offset_fields = [work.fields(state) for state in offset_states]

    own_place = source_place(me)
    first_side = jnp.broadcast_to(jnp.full((1, 1), 1.0, jnp.float32) * side.astype(jnp.float32), (chunk_rows, LANES)) < 0.5
    before, after = own_place < 0.0, own_place > TEAM - 1.0
    use_chosen = jnp.logical_or(jnp.logical_and(first_side, before), jnp.logical_and(jnp.logical_not(first_side), after))
    use_far = jnp.logical_and(jnp.logical_or(before, after), jnp.logical_not(use_chosen))

    def arrived_far():
        remote(cand.at[TEAM + 1], cand.at[TEAM + 1], whole_sem.at[1], far_from).wait_recv()

    pl.when(takes_far)(arrived_far)
    pieces = []
    for chunk in range(chunks):
        def arrived():
            remote(chosen.at[chunk], cand.at[TEAM, chunk], chosen_sem.at[chunk], chosen_from).wait_recv()

        pl.when(takes_chosen)(arrived)
        value = team_value(own_place, chunk)
        value = jnp.where(use_chosen, cand[TEAM, chunk], value)
        pieces.append(jnp.where(use_far, cand[TEAM + 1, chunk], value))
    present = [jnp.concatenate(pieces[part * per_part : (part + 1) * per_part], axis=0) for part in range(PARTS)]

    moved = present
    for move in range(len(drift)):
        candidate = [work.keep * moved[part] + drift[move][part] for part in range(PARTS)]
        moved = [jnp.where(taken[move], candidate[part], moved[part]) for part in range(PARTS)]
    for part in range(PARTS):
        moved_stage[0, part] = moved[part]
    leave = pltpu.make_async_copy(moved_stage, moved_ref, load_sem)
    leave.start()

    base_state = work.folded(present)
    base_fields = work.fields(base_state)
    states = [gain * base_state + state for gain, state in zip(gains, offset_states)]
    fields = [gain * base_fields + value for gain, value in zip(gains, offset_fields)]
    for move, score in enumerate(work.scores(states, fields, observed_ref)):
        misfit_ref[0, move] = score

    leave.wait()
    for copies in stages:
        for copy in copies:
            copy.wait_send()
    to_sibling.wait_send()
    pl.when(sends_far)(to_far.wait_send)
    for chunk in range(chunks):
        cross(place, chunk).wait_send()
        relay(across, chunk).wait_send()
        pl.when(sends_chosen)(forward(chunk).wait_send)


def halves(table):
    table = np.asarray(table, np.float64)
    high = table.astype(np.float32).astype(ml_dtypes.bfloat16)
    rest = (table - high.astype(np.float64)).astype(np.float32).astype(ml_dtypes.bfloat16)
    return np.stack([high, rest])


def make_tables(grid):
    half = grid // 2
    angle = 2.0 * math.pi / grid
    index = np.arange(grid)
    low = np.arange(half)
    phase = (index[:, None] * low[None, :] % grid) * angle
    sines = np.sin(phase)
    sines[:, 0] = 1.0 - 2.0 * (index % 2)
    fold = np.concatenate([np.cos(phase), sines], axis=1)
    weight = np.where(low == 0, 1.0, 2.0)[:, None]
    back = np.concatenate([weight * np.cos(phase).T, -weight * np.sin(phase).T], axis=0) / spectral_scale
    fore = np.concatenate([np.cos(phase), -np.sin(phase)], axis=1) * (spectral_scale / (grid * grid))
    flip = np.zeros((half, half))
    flip[low, (half - low) % half] = 1.0
    wave_y = np.concatenate([low, np.where(low == 0, half, low)]).astype(np.float64)[:, None]
    wave_x = low.astype(np.float64)[None, :]
    square = wave_y**2 + wave_x**2
    inverse = np.where(square > 0, 1.0 / np.maximum(square, 1.0), 0.0)
    damping = 1.0 / (1.0 + time_step * viscosity * square)
    keeper = (np.abs(wave_y) <= grid // 3) & (wave_x <= grid // 3)
    doubled = np.where(np.concatenate([low, low])[:, None] == 0, 1.0, 2.0)
    flux = -time_step * keeper * doubled * damping
    signed = np.where(index < half, index, index - grid).astype(np.float64)[:, None]
    prior = prior_amplitude / (1.0 + np.sqrt(signed**2 + wave_x**2) / 8.0)
    scales = np.stack([inverse, damping, flux, step_size * prior]).astype(np.float32)
    return (
        halves(fold), halves(fold.T), halves(back), halves(fore),
        flip.astype(ml_dtypes.bfloat16), scales,
    )


def split(value):
    high = value.astype(jnp.bfloat16)
    return high, (value - high.astype(jnp.float32)).astype(jnp.bfloat16)


def dot(a, b):
    return jnp.dot(a, b, preferred_element_type=jnp.float32)


def table_left(table, value):
    high, rest = split(value)
    return dot(table[0], high) + dot(table[0], rest) + dot(table[1], high)


def table_right(value, table):
    high, rest = split(value)
    return dot(high, table[0]) + dot(rest, table[0]) + dot(high, table[1])


class Work:
    def __init__(self, devices, grid, tables):
        fold, unfold, back, fore, flip, scales = tables
        self.devices, self.grid, self.half = devices, grid, grid // 2
        self.fold = (fold[0], fold[1])
        self.unfold = (unfold[0], unfold[1])
        self.back = (back[0], back[1])
        self.fore = (fore[0], fore[1])
        self.flip = flip[...]
        self.scales = scales
        self.keep = math.sqrt(1.0 - step_size * step_size)
        row_ids = lax.broadcasted_iota(jnp.int32, (self.half, grid), 0)
        self.first = row_ids == 0
        self.wave = row_ids.astype(jnp.float32)
        self.wave_x = lax.broadcasted_iota(jnp.int32, (grid, self.half), 1).astype(jnp.float32)

    def wide(self, index):
        value = self.scales[index]
        return jnp.concatenate([value, value], axis=1)

    def turn(self, value):
        return jnp.concatenate([-value[:, self.half :], value[:, : self.half]], axis=1)

    def drifts(self, noise_ref, totals):
        half_low = LOW // 2
        lanes = lax.broadcasted_iota(jnp.int32, (half_low, self.half), 1)
        prior = self.scales[3]
        inner = slice(half_low, self.grid - half_low)
        spreads = []
        for part in range(PARTS):
            head, tail = [
                step_size * jnp.sqrt(total * (1.0 / self.devices) + 1e-06)
                for total in totals[2 * part : 2 * part + 2]
            ]
            top = jnp.where(lanes < LOW, head, prior[:half_low])
            bottom = jnp.where(lanes < LOW, tail, prior[self.grid - half_low :])
            spreads.append(jnp.concatenate([top, prior[inner], bottom], axis=0))
        return [
            [spreads[part] * noise_ref[move, 0, part] for part in range(PARTS)]
            for move in range(noise_ref.shape[0])
        ]

    def unrolled(self, drift, taken):
        gain, offset = 1.0, [jnp.zeros_like(value) for value in drift[0]]
        gains, offsets = [], []
        for step, accepted in zip(drift, taken):
            new_gain = self.keep * gain
            new_offset = [self.keep * old + value for old, value in zip(offset, step)]
            gains.append(new_gain)
            offsets.append(new_offset)
            gain = jnp.where(accepted, new_gain, gain)
            offset = [jnp.where(accepted, new, old) for new, old in zip(new_offset, offset)]
        return gains, offsets

    def folded(self, parts):
        half = self.half
        top = jnp.concatenate([part[:half] for part in parts], axis=1)
        high, rest = split(jnp.concatenate([part[half:] for part in parts], axis=1))
        other = dot(self.flip, high) + dot(self.flip, rest)
        even = top + jnp.where(self.first, 0.0, other)
        odd = jnp.where(self.first, other, self.turn(top - other))
        return jnp.concatenate([even, odd], axis=0)

    def fields(self, state):
        half, wave_x = self.half, self.wave_x
        psi = state * self.wide(0)
        even, odd = psi[:half], psi[half:]
        along_y = jnp.concatenate(
            [self.wave * odd, jnp.where(self.first, -float(half) * self.turn(odd), -self.wave * even)], axis=0
        )
        along_x = jnp.concatenate([wave_x * psi[:, half:], -wave_x * psi[:, :half]], axis=1)
        rows = [table_left(self.fold, value) for value in (state, along_y, along_x)]
        return table_right(jnp.concatenate(rows, axis=0), self.back)

    def scores(self, states, fields, observed_ref):
        grid, half, wave, wave_x = self.grid, self.half, self.wave, self.wave_x
        products = []
        for value in fields:
            vort = value[:grid]
            products += [value[grid : 2 * grid] * vort, value[2 * grid :] * vort]
        rows = table_right(jnp.concatenate(products, axis=0), self.fore)
        damping, flux_scale = self.wide(1), self.wide(2)
        finals = []
        for move, state in enumerate(states):
            flux_u = table_left(self.unfold, rows[(2 * move) * grid : (2 * move + 1) * grid])
            flux_v = table_left(self.unfold, rows[(2 * move + 1) * grid : (2 * move + 2) * grid])
            along_x = jnp.concatenate([-wave_x * flux_u[:, half:], wave_x * flux_u[:, :half]], axis=1)
            along_y = jnp.concatenate([wave * flux_v[half:], -wave * flux_v[:half]], axis=0)
            finals.append(table_left(self.fold, state * damping + flux_scale * (along_x + along_y)))
        forecast = table_right(jnp.concatenate(finals, axis=0), self.back)
        scale = 1.0 / (2.0 * noise_level * noise_level * grid * grid)
        result = []
        for move in range(len(states)):
            gap = forecast[move * grid : (move + 1) * grid] - observed_ref[...]
            result.append(jnp.sum(gap * gap) * scale)
        return result


def body(devices, particles, offspring, noise, accept, observed):
    groups = split_bits(devices)
    _, _, grid, half = particles.shape
    moves = noise.shape[0]
    assert particles.shape[0] == 1 and half == LANES and devices <= LOW // 2 * (LANES - COUNT_LANE)
    copies = sum((1 << width) - 1 for _, width in groups)
    package = LOW // 2
    assert 2 * PARTS * LOW == COUNT_LANE
    slots = TEAM + 2
    assert devices % TEAM == 0 and (PARTS * grid) % CHUNKS == 0
    chunk_shape = (CHUNKS, PARTS * grid // CHUNKS, half)
    tables = [jnp.asarray(table) for table in make_tables(grid)]
    hbm = pl.BlockSpec(memory_space=HBM)
    smem = pl.BlockSpec(memory_space=pltpu.SMEM)
    fetched = [noise, observed] + tables
    moved, misfit = pl.pallas_call(
        functools.partial(filter_kernel, devices, groups),
        out_shape=(
            jax.ShapeDtypeStruct((1, PARTS, grid, half), jnp.float32),
            jax.ShapeDtypeStruct((1, moves), jnp.float32),
        ),
        in_specs=[hbm, smem, smem] + [hbm] * len(fetched),
        out_specs=(hbm, smem),
        scratch_shapes=[
            pltpu.VMEM((slots,) + chunk_shape, jnp.float32),
            pltpu.VMEM(chunk_shape, jnp.float32),
            pltpu.VMEM((len(groups) + 1, package, LANES), jnp.float32),
            pltpu.VMEM((copies, package, LANES), jnp.float32),
            pltpu.VMEM((1, PARTS, grid, half), jnp.float32),
        ]
        + [pltpu.VMEM(value.shape, value.dtype) for value in fetched]
        + [
            pltpu.SemaphoreType.DMA,
            pltpu.SemaphoreType.DMA((2, 2)),
            pltpu.SemaphoreType.DMA((CHUNKS, 2)),
            pltpu.SemaphoreType.DMA((CHUNKS, 2)),
            pltpu.SemaphoreType.DMA((CHUNKS, 2)),
            pltpu.SemaphoreType.DMA((copies,)),
            pltpu.SemaphoreType.DMA((copies,)),
            pltpu.SemaphoreType.DMA((len(fetched),)),
        ],
        compiler_params=pltpu.CompilerParams(
            collective_id=0, has_side_effects=True, vmem_limit_bytes=63 * 1024 * 1024
        ),
        name="filter",
    )(particles.reshape(chunk_shape), offspring, accept.T, *fetched)
    return moved, misfit.T


def solution(mesh):
    return jax.shard_map(
        functools.partial(body, mesh.shape["dom"]),
        mesh=mesh,
        in_specs=(
            P("dom", None, None, None),
            P("dom"),
            P(None, "dom", None, None, None),
            P(None, "dom"),
            P(),
        ),
        out_specs=(P("dom", None, None, None), P(None, "dom")),
        check_vma=False,
    )
```
